32 devices in a mesh: groups: 2 (over x), expert: 16 (over z, y, core).
Axes of the slice: x: 2, y: 2, z: 4, core: 2. Of those that a mesh axis runs over, the one named last changes fastest.
Arguments:
- tokens: bfloat16 [2048, 4096], P(('groups', 'expert')), parts along dimension 0, may hold values from -6 to 6
- out_grad: bfloat16 [2048, 4096], P(('groups', 'expert')), parts along dimension 0, may hold values from -6 to 6
- routes: int32 [2048, 8], P(('groups', 'expert')), parts along dimension 0, may hold values from 0 to 31, all different within a row; in each aligned block of 64 rows (0 to 63, 64 to 127, ...) at most 24 rows name the same one
- route_weight: float32 [2048, 8], P(('groups', 'expert')), parts along dimension 0, may hold values from 0.05 to 1
- example_ids: int32 [32, 64], P(('groups', 'expert')), parts along dimension 0, may hold values from 0 to 3, never falling along the last dimension, each value on 1 to 32 neighbouring positions
- in_proj: bfloat16 [32, 4096, 64], P('expert'), may hold values from -0.09375 to 0.09375
- out_proj: bfloat16 [4096, 64], replicated, may hold values from -0.09375 to 0.09375
- queries: bfloat16 [256, 4096], P('expert'), may hold values from -0.29882812 to 0.29882812
Outputs:
- sketches: float32 [128, 4096], P(('groups', 'expert')), parts along dimension 0
- scores: float32 [128, 256], P(('groups', 'expert')), parts along dimension 0
The draws below stay inside these ranges and needn't reach their ends.
There are 2 independent parts, one for each index of `groups`. The reference program is written for one: setup_inputs(seed, part) draws one part's arguments, and reference() takes and returns one part's arrays. A program takes and returns all parts, laid end to end along the dimension named above; an argument that names none is the same for every part. Nothing has to cross between parts.
Inputs may be any that keep to these rules, and one draw needn't show every extreme that they name: The 8 experts of a token differ. Among the 64 tokens of one device no expert is named by more than 24 routes, a bound that some block reaches. `example_ids`: on each device the ids never fall along the tokens, every id occurs, and one example holds exactly 32 tokens.
All inputs are finite; a program needn't handle non-finite values.
Results may differ from the reference program's by a relative error of at most 0.0042.
Values may be sent and summed in bfloat16 or wider, within the bound.
No kernel may reach another device: no remote copies, remote signals or barrier semaphores. Data moves between devices by JAX's collectives and lax.ppermute only.
A program may use at most 128 MiB of HBM per device.

```python
import math
import jax
import jax.numpy as jnp
import numpy as np
from jax import lax

D = 4096
TOP = 8
RANK = 64
TOK_DEV = 64
EX_DEV = 4
EXPERTS = 32
SK = 4096
SHARDS = 16
TOKENS = 1024
EXAMPLES = 64
QUERIES = 256
CAP = 24
SEG_MOST = 32
N_EXPERT = 16


def steps_of(key, extent, split, least, top_value):
    level = 1.0
    for position, parts in split:
        heights = jax.random.uniform(jax.random.fold_in(jax.random.fold_in(key, 6), position), (parts,), jnp.float32, least / len(split), top_value / len(split))
        level = level * jnp.repeat(jnp.exp(heights), extent[position] // parts).reshape((-1,) + (1,) * (len(extent) - 1 - position))
    return level


def length_profile(number_of, total, reach, slope):
    weights = [(1 << 20) // math.isqrt(standing ** slope) + 1 for standing in range(2, number_of + 1)]
    surplus, holding = total - reach - (number_of - 1), [1] * (number_of - 1)
    while surplus > 0:
        free = [i for i in range(number_of - 1) if holding[i] < reach]
        pool, remaining = sum([weights[i] for i in free]), surplus
        for i in free:
            extra = min(reach - holding[i], max(1, remaining * weights[i] // pool), surplus)
            holding[i] = holding[i] + extra
            surplus = surplus - extra
    return np.array([reach] + holding)


def ragged(stream_key, amount, total, most, skew):
    if amount == 2:
        one = jax.random.randint(stream_key, (), max(1, total - most), min(most, total - 1) + 1)
        return jnp.stack([one, total - one])
    sizes = jnp.asarray(length_profile(amount, total, most, skew), jnp.int32)
    twos = (amount - 1) // 2
    source_of, taker = sizes[1:1 + 2 * twos:2], sizes[2:2 + 2 * twos:2]
    margin = jnp.minimum(source_of - 1, most - taker)
    shifted = jax.random.randint(jax.random.fold_in(stream_key, 1), (twos,), 0, 1 << 20) % (margin + 1)
    sizes = sizes.at[1:1 + 2 * twos:2].set(source_of - shifted).at[2:2 + 2 * twos:2].set(taker + shifted)
    return sizes[jax.random.permutation(jax.random.fold_in(stream_key, 2), amount)]


def assign_block(rng, own, number, rows, number_of, top, most, skew):
    sequence = jax.random.permutation(rng, number_of)
    crowded, usual = portions_of(number_of, rows * top, most, skew, True), portions_of(number_of, rows * top, most, skew, False)
    places = jnp.arange(number_of)

    def named(sizes, rotation):
        used = int((sizes > 0).sum())
        fixed = max(1, used // 4)
        passed = fixed + (places - fixed + rotation * (used - fixed)) % max(1, number_of - fixed)
        return jnp.zeros((number_of,), jnp.int32).at[sequence[jnp.where(places < fixed, places, passed)]].set(jnp.asarray(sizes, jnp.int32))

    sizes = jnp.where(number % 4 == 0, named(crowded, number // 4), named(usual, number - number // 4 - 1))
    mixed = jax.random.permutation(jax.random.fold_in(own, 3), number_of)
    source_of, sink = mixed[0:number_of // 2 * 2:2], mixed[1:number_of // 2 * 2:2]
    slack = jnp.minimum(sizes[source_of] - 1, most - sizes[sink]) // 2
    slack = jnp.where((source_of == sequence[0]) | (sink == sequence[0]) | (sizes[sink] == 0), 0, jnp.maximum(slack, 0))
    passed = jax.random.randint(jax.random.fold_in(own, 4), (number_of // 2,), 0, 1 << 20) % (slack + 1)
    sizes = sizes.at[source_of].add(-passed).at[sink].add(passed)
    members = jnp.searchsorted(jnp.cumsum(sizes), jnp.arange(rows * top), side="right").astype(jnp.int32)
    grid = members.reshape(top, rows).T
    grid = grid[jax.random.permutation(jax.random.fold_in(own, 1), rows)]
    rotation = jax.random.randint(jax.random.fold_in(own, 2), (rows, 1), 0, top)
    return jnp.take_along_axis(grid, (jnp.arange(top)[None, :] + rotation) % top, axis=1)


def portions_of(number_of, total, bound, slope, full):
    portions = [(1 << 20) // math.isqrt(rank ** slope) + 1 for rank in range(1, number_of + 1)]
    largest = bound if full else min(bound, max(-(-total // number_of), total * portions[0] // sum(portions)))
    least = 1 if total - largest >= number_of - 1 else 0
    holding, surplus = [largest] + [least] * (number_of - 1), total - largest - least * (number_of - 1)
    while surplus > 0:
        free = [i for i in range(1, number_of) if holding[i] < largest] or [i for i in range(1, number_of) if holding[i] < bound]
        whole, budget = sum([portions[i] for i in free]), surplus
        for i in free:
            addition = min(bound - holding[i], max(1, budget * portions[i] // whole), surplus)
            holding[i] = holding[i] + addition
            surplus = surplus - addition
    return np.array(holding)


def centred(own_key, shape, scale, limit, split=(), held_as=jnp.bfloat16):
    entries = scale * jax.random.normal(own_key, shape, jnp.float32)
    if split:
        entries = entries * steps_of(own_key, shape, split, -0.22, 0.18)
    return jnp.clip(entries, -limit, limit).astype(held_as)


def setup_inputs(seed: int = 0, part: int = 0) -> dict:
    streams_of = jax.random.split(jax.random.key(seed), 9)
    own_keys = jax.random.split(jax.random.fold_in(streams_of[8], part), 9)
    tokens = centred(own_keys[0], (TOKENS, D), 1.0, 6.0, ((0, 16),))
    out_grad = centred(own_keys[1], (TOKENS, D), 1.0, 6.0, ((0, 16),))
    routes_keys = jax.random.split(jax.random.fold_in(own_keys[2], 1), TOKENS // TOK_DEV)
    routes_turns = jax.random.permutation(jax.random.fold_in(own_keys[2], 3), TOKENS // TOK_DEV)
    routes = jax.vmap(lambda own, number: assign_block(jax.random.fold_in(own_keys[2], 2), own, number, TOK_DEV, EXPERTS, TOP, CAP, 2))(routes_keys, routes_turns).reshape((TOKENS, TOP))
    route_weight = jnp.clip(jnp.exp(math.log(1.0) - 2.9957323 * jax.random.uniform(own_keys[3], (TOKENS, TOP), jnp.float32) ** steps_of(own_keys[3], (TOKENS, TOP), ((0, 16),), -0.2, 0.2)), 0.05, 1.0)
    example_ids = jax.vmap(lambda own: jnp.searchsorted(jnp.cumsum(ragged(own, EX_DEV, TOK_DEV, SEG_MOST, 1)), jnp.arange(TOK_DEV), side="right"))(jax.random.split(own_keys[4], SHARDS)).reshape((SHARDS, TOK_DEV)).astype(jnp.int32)
    in_proj = centred(streams_of[5], (EXPERTS, D, RANK), D ** -0.5, 0.09375, ((0, 16),))
    out_proj = centred(streams_of[6], (D, RANK), D ** -0.5, 0.09375)
    queries = centred(streams_of[7], (QUERIES, SK), 0.05, 0.29882812, ((0, 16),))
    return dict(tokens=tokens, out_grad=out_grad, routes=routes, route_weight=route_weight, example_ids=example_ids, in_proj=in_proj, out_proj=out_proj, queries=queries)


def reference(tokens, out_grad, routes, route_weight, example_ids, in_proj, out_proj, queries):
    token_total = tokens.shape[0]
    flat_routes = routes.reshape(-1)
    row_total = flat_routes.shape[0]
    row_limit = N_EXPERT * CAP

    def per_expert(expert_id):
        row_index = jnp.nonzero(flat_routes == expert_id, size=row_limit, fill_value=row_total)[0].astype(jnp.int32)
        token_index = jnp.minimum(row_index // TOP, token_total - 1)
        projected = jnp.dot(tokens[token_index], in_proj[expert_id], preferred_element_type=jnp.float32)
        return row_index, projected

    row_index, projected = lax.map(per_expert, jnp.arange(EXPERTS, dtype=jnp.int32))
    input_side = jnp.zeros((row_total, RANK), jnp.float32)
    input_side = input_side.at[row_index.reshape(-1)].set(projected.reshape(-1, RANK), mode="drop")
    grad_side = jnp.dot(out_grad, out_proj, preferred_element_type=jnp.float32)
    weighted = (route_weight[:, :, None] * grad_side[:, None, :]).astype(jnp.bfloat16)
    weighted = lax.optimization_barrier(weighted).astype(jnp.float32)
    weighted = weighted.reshape(N_EXPERT, TOK_DEV * TOP, RANK)
    input_dev = input_side.reshape(N_EXPERT, TOK_DEV * TOP, RANK)

    def per_device(pieces):
        rows_input, rows_weighted, device_ids = pieces
        member = (device_ids[:, None] == jnp.arange(EX_DEV, dtype=jnp.int32)[None, :]).astype(jnp.float32)
        counts = jnp.sum(member, axis=0)
        row_member = jnp.repeat(member, TOP, axis=0)
        spread = (row_member[:, :, None] * rows_input[:, None, :]).reshape(-1, EX_DEV * RANK)
        summed = jnp.dot(spread.T, rows_weighted, precision=lax.Precision.HIGHEST, preferred_element_type=jnp.float32)
        return summed.reshape(EX_DEV, RANK * RANK) / counts[:, None]

    sketches = lax.map(per_device, (input_dev, weighted, example_ids)).reshape(EXAMPLES, RANK * RANK)
    rounded = sketches.astype(jnp.bfloat16)
    scores = jnp.dot(rounded, queries.T, preferred_element_type=jnp.float32)
    return sketches, scores
```

```python
import jax
import jax.numpy as jnp
from jax import lax
from jax.sharding import PartitionSpec as P

RANK = 64
EX_DEV = 4


def shards(tokens, out_grad, routes, route_weight, example_ids, in_proj, out_proj, queries):
    token_count, model_width = tokens.shape
    owned = in_proj.shape[0]
    n = lax.axis_size("expert")
    experts_all = owned * n
    everyone = lax.all_gather(tokens, "expert", axis=0, tiled=True)
    all_queries = lax.all_gather(queries, "expert", axis=0, tiled=True)
    weights = jnp.swapaxes(in_proj, 1, 2).reshape(owned * RANK, model_width)
    projected = lax.dot_general(
        everyone, weights, (((1,), (1,)), ((), ())), preferred_element_type=jnp.float32
    ).astype(jnp.bfloat16)
    returned = lax.all_to_all(
        projected.reshape(n, token_count, owned * RANK), "expert", split_axis=0, concat_axis=0, tiled=True
    )
    grad_side = jnp.dot(out_grad, out_proj, preferred_element_type=jnp.float32)
    hit = routes[:, :, None] == jnp.arange(experts_all, dtype=jnp.int32)[None, None, :]
    gate = jnp.sum(jnp.where(hit, route_weight[:, :, None], 0.0), axis=1)
    local_ids = example_ids.reshape(token_count)
    member = (local_ids[:, None] == jnp.arange(EX_DEV, dtype=jnp.int32)[None, :]).astype(jnp.float32)
    counts = jnp.sum(member, axis=0)
    weighted = (gate.T[:, :, None] * grad_side[None, :, :]).astype(jnp.bfloat16)
    widened = jnp.where(member.T[None, :, :, None].transpose(0, 2, 1, 3) > 0, weighted[:, :, None, :], jnp.zeros((), jnp.bfloat16))
    widened = widened.reshape(experts_all * token_count, EX_DEV * RANK)
    sides = returned.reshape(n, token_count, owned, RANK).transpose(0, 2, 1, 3).reshape(experts_all * token_count, RANK)
    block_sum = lax.dot_general(
        sides, widened, (((0,), (0,)), ((), ())), preferred_element_type=jnp.float32
    )
    combined = block_sum.reshape(RANK, EX_DEV, RANK).transpose(1, 0, 2).reshape(EX_DEV, RANK * RANK)
    sketches = combined / counts[:, None]
    scores = lax.dot_general(
        sketches.astype(jnp.bfloat16), all_queries, (((1,), (1,)), ((), ())), preferred_element_type=jnp.float32
    )
    return (sketches, scores)


def solution(mesh):
    placed = (
        P(("groups", "expert"), None),
        P(("groups", "expert"), None),
        P(("groups", "expert"), None),
        P(("groups", "expert"), None),
        P(("groups", "expert"), None),
        P("expert", None, None),
        P(),
        P("expert", None),
    )
    return jax.shard_map(
        shards,
        mesh=mesh,
        in_specs=placed,
        out_specs=(P(("groups", "expert"), None), P(("groups", "expert"), None)),
        check_vma=False,
    )
```

```python
import functools

import jax
import jax.numpy as jnp
from jax import lax
from jax.experimental import pallas as pl
from jax.experimental.pallas import tpu as pltpu
from jax.sharding import PartitionSpec as P

RANK = 64
EX_DEV = 4
QUAD = 4

NT = (((1,), (1,)), ((), ()))
TN = (((0,), (0,)), ((), ()))


def combine_kernel(blocks, experts, first, last, *refs):
    sides, wide = refs[:blocks], refs[blocks]
    total = jnp.zeros((RANK, EX_DEV * RANK), jnp.float32) if first else refs[blocks + 1][...]
    out = refs[-1]
    for b in range(blocks):
        for e in range(experts):
            total += lax.dot_general(
                sides[b][:, e * RANK : (e + 1) * RANK],
                wide[b * experts + e],
                TN,
                preferred_element_type=jnp.float32,
            )
    if last:
        counts = refs[-2]
        for x in range(EX_DEV):
            out[x] = total[:, x * RANK : (x + 1) * RANK] / counts[x : x + 1, :]
    else:
        out[...] = total


def combine(sides, wide, total=None, counts=None):
    experts = wide.shape[0] // len(sides)
    extra = [a for a in (total, counts) if a is not None]
    shape = (RANK, EX_DEV * RANK) if counts is None else (EX_DEV, RANK, RANK)
    return pl.pallas_call(
        functools.partial(combine_kernel, len(sides), experts, total is None, counts is not None),
        out_shape=jax.ShapeDtypeStruct(shape, jnp.float32),
        in_specs=[pl.BlockSpec(memory_space=pltpu.VMEM)] * (len(sides) + 1 + len(extra)),
        out_specs=pl.BlockSpec(memory_space=pltpu.VMEM),
        compiler_params=pltpu.CompilerParams(vmem_limit_bytes=32 << 20),
        name="combine",
    )(*sides, wide, *extra)


def shards(tokens, out_grad, routes, route_weight, example_ids, in_proj, out_proj, queries):
    token_count, model_width = tokens.shape
    owned = in_proj.shape[0]
    n = lax.axis_size("expert")
    planes = n // QUAD
    me = lax.axis_index("expert")
    plane, spot = me // QUAD, me % QUAD

    def move(array, hops):
        pairs = [(a * QUAD + q, b * QUAD + q) for a, b in hops for q in range(QUAD)]
        return lax.ppermute(array, "expert", pairs)

    def swap(array, bit):
        return lax.ppermute(array, "expert", [(i, i ^ bit) for i in range(n)])

    weights = jnp.swapaxes(in_proj, 1, 2).reshape(owned * RANK, model_width)

    up, down = tokens, tokens
    arrived = []
    over_y = swap(weights, 2)
    for s in range(1, planes):
        up_hops = [(p, p + 1) for p in range(s - 1, planes - 1)]
        down_hops = [(p, p - 1) for p in range(1, planes - s + 1)]
        up_ok, down_ok = plane >= s, plane < planes - s
        up_home = [(p, p - s) for p in range(s, planes)]
        down_home = [(p, p + s) for p in range(planes - s)]
        if 2 * s > planes + 1:
            up = down = move(up, up_hops + down_hops)
        else:
            up, down = move(up, up_hops), move(down, down_hops)
            if 2 * s >= planes:
                up = down = up + down
        if 2 * s >= planes:
            origin = jnp.where(up_ok, plane - s, jnp.where(down_ok, plane + s, -1))
            arrived.append((up, origin, up_home + down_home))
        else:
            arrived.append((up, jnp.where(up_ok, plane - s, -1), up_home))
            arrived.append((down, jnp.where(down_ok, plane + s, -1), down_home))
    over_core = swap(weights, 1)
    across = swap(over_y, 1)
    all_queries = lax.all_gather(queries, "expert", axis=0, tiled=True)
    quad_weights = jnp.concatenate([weights, over_core, over_y, across], axis=0)

    def project(block):
        return lax.dot_general(block, quad_weights, NT, preferred_element_type=jnp.float32).astype(jnp.bfloat16)

    returned, homes = [], []
    own = project(tokens)
    for block, origin, home in arrived:
        returned.append(move(project(block), home))
        back = -jnp.ones((), jnp.int32)
        for a, b in home:
            back = jnp.where(plane == b, a, back)
        homes.append(back)

    grad_side = jnp.dot(out_grad, out_proj, preferred_element_type=jnp.float32)
    rel = jnp.arange(QUAD, dtype=jnp.int32)
    inner = ((spot ^ rel)[:, None] * owned + jnp.arange(owned, dtype=jnp.int32)[None, :]).reshape(-1)
    place = jnp.stack([plane] + homes)
    expert_ids = jnp.where(place[:, None] >= 0, place[:, None] * (QUAD * owned) + inner[None, :], -1).reshape(-1)
    gate = jnp.sum(
        jnp.where(routes.T[None, :, :] == expert_ids[:, None, None], route_weight.T[None, :, :], 0.0), axis=1
    )
    local_ids = example_ids.reshape(token_count)
    member = local_ids[:, None] == jnp.arange(EX_DEV, dtype=jnp.int32)[None, :]
    counts = jnp.sum(member.astype(jnp.float32), axis=0)
    counts = jnp.broadcast_to(counts[:, None], (EX_DEV, RANK))
    repeated = jnp.concatenate([grad_side] * EX_DEV, axis=1)
    widely = jnp.repeat(member, RANK, axis=1)
    wide = jnp.where(
        widely[None], (gate[:, :, None] * repeated[None]).astype(jnp.bfloat16), jnp.zeros((), jnp.bfloat16)
    )
    experts = QUAD * owned
    early = combine([own] + returned[:-1], wide[:-experts])
    sketches = combine([returned[-1]], wide[-experts:], early, counts)
    sketches = sketches.reshape(EX_DEV, RANK * RANK)
    scores = lax.dot_general(sketches.astype(jnp.bfloat16), all_queries, NT, preferred_element_type=jnp.float32)
    return (sketches, scores)


def solution(mesh):
    placed = (
        P(("groups", "expert"), None),
        P(("groups", "expert"), None),
        P(("groups", "expert"), None),
        P(("groups", "expert"), None),
        P(("groups", "expert"), None),
        P("expert", None, None),
        P(),
        P("expert", None),
    )
    return jax.shard_map(
        shards,
        mesh=mesh,
        in_specs=placed,
        out_specs=(P(("groups", "expert"), None), P(("groups", "expert"), None)),
        check_vma=False,
    )
```

```python
import functools

import jax
import jax.numpy as jnp
from jax import lax
from jax.experimental import pallas as pl
from jax.experimental.pallas import tpu as pltpu
from jax.sharding import PartitionSpec as P

RANK = 64
EX_DEV = 4
QUAD = 4

NT = (((1,), (1,)), ((), ()))
TN = (((0,), (0,)), ((), ()))


def combine_kernel(blocks, experts, first, last, *refs):
    sides, wide = refs[:blocks], refs[blocks]
    total = jnp.zeros((RANK, EX_DEV * RANK), jnp.float32) if first else refs[blocks + 1][...]
    out = refs[-1]
    for b in range(blocks):
        for e in range(experts):
            total += lax.dot_general(
                sides[b][:, e * RANK : (e + 1) * RANK],
                wide[b * experts + e],
                TN,
                preferred_element_type=jnp.float32,
            )
    if last:
        counts = refs[-2]
        for x in range(EX_DEV):
            out[x] = total[:, x * RANK : (x + 1) * RANK] / counts[x : x + 1, :]
    else:
        out[...] = total


def combine(sides, wide, total=None, counts=None):
    experts = wide.shape[0] // len(sides)
    extra = [a for a in (total, counts) if a is not None]
    shape = (RANK, EX_DEV * RANK) if counts is None else (EX_DEV, RANK, RANK)
    return pl.pallas_call(
        functools.partial(combine_kernel, len(sides), experts, total is None, counts is not None),
        out_shape=jax.ShapeDtypeStruct(shape, jnp.float32),
        in_specs=[pl.BlockSpec(memory_space=pltpu.VMEM)] * (len(sides) + 1 + len(extra)),
        out_specs=pl.BlockSpec(memory_space=pltpu.VMEM),
        compiler_params=pltpu.CompilerParams(vmem_limit_bytes=32 << 20),
        name="combine",
    )(*sides, wide, *extra)


def assemble_kernel(planes, groups, here_ref, mine_ref, over_y_ref, rest_ref, out_ref):
    span = mine_ref.shape[0]
    rows, columns = span // planes, out_ref.shape[1] // groups
    sources = (mine_ref, rest_ref, over_y_ref, rest_ref)
    for rel in range(QUAD):
        base = span if rel == 3 else 0
        for d in range(planes):
            home = lax.rem(here_ref[0] + (planes - d), planes) * QUAD + (here_ref[1] ^ rel)
            row = pl.multiple_of(home * rows, rows)
            for k in range(groups):
                column = pl.multiple_of(lax.rem(here_ref[2] + (groups - k), groups) * columns, columns)
                out_ref[pl.ds(row, rows), pl.ds(column, columns)] = sources[rel][
                    base + d * rows : base + (d + 1) * rows, k * columns : (k + 1) * columns
                ]


def assemble(here, mine, over_y, rest, planes, groups):
    span, width = mine.shape
    vmem = pl.BlockSpec(memory_space=pltpu.VMEM)
    return pl.pallas_call(
        functools.partial(assemble_kernel, planes, groups),
        out_shape=jax.ShapeDtypeStruct((span * QUAD, width), mine.dtype),
        in_specs=[pl.BlockSpec(memory_space=pltpu.SMEM), vmem, vmem, vmem],
        out_specs=vmem,
        compiler_params=pltpu.CompilerParams(vmem_limit_bytes=32 << 20),
        name="assemble",
    )(here, mine, over_y, rest)


def after(array, *others):
    return lax.optimization_barrier((array, *others))[0]


def shards(tokens, out_grad, routes, route_weight, example_ids, in_proj, out_proj, queries):
    token_count, model_width = tokens.shape
    owned = in_proj.shape[0]
    n, groups = lax.axis_size("expert"), lax.axis_size("groups")
    planes = n // QUAD
    me, group = lax.axis_index("expert"), lax.axis_index("groups")
    plane, spot = me // QUAD, me % QUAD

    def move(array, hops):
        pairs = [(a * QUAD + q, b * QUAD + q) for a, b in hops for q in range(QUAD)]
        return lax.ppermute(array, "expert", pairs)

    def swap(array, bit):
        return lax.ppermute(array, "expert", [(i, i ^ bit) for i in range(n)])

    up, down = tokens, tokens
    arrived, steps = [], []
    for s in range(1, planes):
        up_hops = [(p, p + 1) for p in range(s - 1, planes - 1)]
        down_hops = [(p, p - 1) for p in range(1, planes - s + 1)]
        up_home = [(p, p - s) for p in range(s, planes)]
        down_home = [(p, p + s) for p in range(planes - s)]
        if 2 * s > planes + 1:
            up = down = move(up, up_hops + down_hops)
        else:
            up, down = move(up, up_hops), move(down, down_hops)
            if 2 * s >= planes:
                up = down = up + down
        steps.append(up)
        if 2 * s >= planes:
            arrived.append((up, up_home + down_home))
        else:
            arrived.extend([(up, up_home), (down, down_home)])

    weights = jnp.swapaxes(in_proj, 1, 2).reshape(owned * RANK, model_width)
    over_y = swap(weights, 2)
    over_core = swap(weights, 1)
    across = swap(after(over_y, steps[1]), 1)
    quad_weights = jnp.concatenate([weights, over_core, over_y, across], axis=0)

    width = queries.shape[1] // groups
    part = lax.dynamic_slice_in_dim(queries, group * width, width, axis=1)
    lined = [part] + [move(part, [(p, (p + d) % planes) for p in range(planes)]) for d in range(1, planes)]
    lined = after(jnp.concatenate(lined, axis=0), steps[0])
    ranged = [lined] + [
        lax.ppermute(lined, "groups", [(g, (g + k) % groups) for g in range(groups)]) for k in range(1, groups)
    ]
    mine = after(jnp.concatenate(ranged, axis=1), steps[1])
    mine_over_y = swap(mine, 2)
    rest = swap(jnp.concatenate([mine, mine_over_y], axis=0), 1)
    here = jnp.stack([plane, spot, group]).astype(jnp.int32)
    all_queries = assemble(here, mine, mine_over_y, rest, planes, groups)

    homes = []
    for _, home in arrived:
        back = -jnp.ones((), jnp.int32)
        for a, b in home:
            back = jnp.where(plane == b, a, back)
        homes.append(back)
    grad_side = jnp.dot(out_grad, out_proj, preferred_element_type=jnp.float32)
    rel = jnp.arange(QUAD, dtype=jnp.int32)
    inner = ((spot ^ rel)[:, None] * owned + jnp.arange(owned, dtype=jnp.int32)[None, :]).reshape(-1)
    place = jnp.stack([plane] + homes)
    expert_ids = jnp.where(place[:, None] >= 0, place[:, None] * (QUAD * owned) + inner[None, :], -1).reshape(-1)
    gate = jnp.sum(
        jnp.where(routes.T[None, :, :] == expert_ids[:, None, None], route_weight.T[None, :, :], 0.0), axis=1
    )
    local_ids = example_ids.reshape(token_count)
    member = local_ids[:, None] == jnp.arange(EX_DEV, dtype=jnp.int32)[None, :]
    counts = jnp.sum(member.astype(jnp.float32), axis=0)
    counts = jnp.broadcast_to(counts[:, None], (EX_DEV, RANK))
    repeated = jnp.concatenate([grad_side] * EX_DEV, axis=1)
    widely = jnp.repeat(member, RANK, axis=1)
    wide = jnp.where(
        widely[None], (gate[:, :, None] * repeated[None]).astype(jnp.bfloat16), jnp.zeros((), jnp.bfloat16)
    )

    def project(block):
        return lax.dot_general(block, quad_weights, NT, preferred_element_type=jnp.float32).astype(jnp.bfloat16)

    experts = QUAD * owned
    returned = [move(project(block), home) for block, home in arrived[:-1]]
    early = combine([project(tokens)] + returned, wide[:-experts])
    block, home = arrived[-1]
    late = move(project(after(block, early)), home)
    sketches = combine([late], wide[-experts:], early, counts)
    sketches = sketches.reshape(EX_DEV, RANK * RANK)
    scores = lax.dot_general(sketches.astype(jnp.bfloat16), all_queries, NT, preferred_element_type=jnp.float32)
    return (sketches, scores)


def solution(mesh):
    placed = (
        P(("groups", "expert"), None),
        P(("groups", "expert"), None),
        P(("groups", "expert"), None),
        P(("groups", "expert"), None),
        P(("groups", "expert"), None),
        P("expert", None, None),
        P(),
        P("expert", None),
    )
    return jax.shard_map(
        shards,
        mesh=mesh,
        in_specs=placed,
        out_specs=(P(("groups", "expert"), None), P(("groups", "expert"), None)),
        check_vma=False,
    )
```

```python
import functools

import jax
import jax.numpy as jnp
from jax import lax
from jax.experimental import pallas as pl
from jax.experimental.pallas import tpu as pltpu
from jax.sharding import PartitionSpec as P

RANK = 64
EX_DEV = 4
QUAD = 4

SMALL = pl.CostEstimate(flops=1024, bytes_accessed=1024, transcendentals=0)

NT = (((1,), (1,)), ((), ()))
TN = (((0,), (0,)), ((), ()))


def combine_kernel(blocks, experts, first, last, *refs):
    sides, wide = refs[:blocks], refs[blocks]
    total = jnp.zeros((RANK, EX_DEV * RANK), jnp.float32) if first else refs[blocks + 1][...]
    out = refs[-1]
    for b in range(blocks):
        for e in range(experts):
            total += lax.dot_general(
                sides[b][:, e * RANK : (e + 1) * RANK],
                wide[b * experts + e],
                TN,
                preferred_element_type=jnp.float32,
            )
    if last:
        counts = refs[-2]
        for x in range(EX_DEV):
            out[x] = total[:, x * RANK : (x + 1) * RANK] / counts[x : x + 1, :]
    else:
        out[...] = total


def combine(sides, wide, total=None, counts=None):
    experts = wide.shape[0] // len(sides)
    extra = [a for a in (total, counts) if a is not None]
    shape = (RANK, EX_DEV * RANK) if counts is None else (EX_DEV, RANK, RANK)
    return pl.pallas_call(
        functools.partial(combine_kernel, len(sides), experts, total is None, counts is not None),
        out_shape=jax.ShapeDtypeStruct(shape, jnp.float32),
        in_specs=[pl.BlockSpec(memory_space=pltpu.VMEM)] * (len(sides) + 1 + len(extra)),
        out_specs=pl.BlockSpec(memory_space=pltpu.VMEM),
        cost_estimate=SMALL,
        compiler_params=pltpu.CompilerParams(vmem_limit_bytes=32 << 20),
        name="combine",
    )(*sides, wide, *extra)


def project_kernel(blocks, *refs):
    parts, weights = refs[:blocks], refs[blocks : blocks + QUAD]
    outs, total = refs[blocks + QUAD : -1], refs[-1]
    rows = parts[0].shape[0]
    depth = 1024
    total[...] = jnp.zeros_like(total)

    @pl.loop(0, parts[0].shape[1] // depth)
    def _(i):
        span = pl.ds(pl.multiple_of(i * depth, depth), depth)
        left = jnp.concatenate([p[:, span] for p in parts], axis=0)
        right = jnp.concatenate([w[:, span] for w in weights], axis=0)
        total[...] += lax.dot_general(left, right, NT, preferred_element_type=jnp.float32)

    for b in range(blocks):
        outs[b][...] = total[b * rows : (b + 1) * rows].astype(jnp.bfloat16)


def project(parts, weights):
    rows, width = parts[0].shape[0], QUAD * weights[0].shape[0]
    vmem = pl.BlockSpec(memory_space=pltpu.VMEM)
    return pl.pallas_call(
        functools.partial(project_kernel, len(parts)),
        out_shape=[jax.ShapeDtypeStruct((rows, width), jnp.bfloat16)] * len(parts),
        in_specs=[vmem] * (len(parts) + QUAD),
        out_specs=[vmem] * len(parts),
        scratch_shapes=[pltpu.VMEM((rows * len(parts), width), jnp.float32)],
        cost_estimate=SMALL,
        compiler_params=pltpu.CompilerParams(vmem_limit_bytes=40 << 20),
        name="project",
    )(*parts, *weights)


def assemble_kernel(planes, groups, here_ref, mine_ref, over_y_ref, rest_ref, out_ref):
    span = mine_ref.shape[0]
    rows, columns = span // planes, out_ref.shape[1] // groups
    sources = (mine_ref, rest_ref, over_y_ref, rest_ref)
    for rel in range(QUAD):
        base = span if rel == 3 else 0
        for d in range(planes):
            home = (here_ref[0] ^ d) * QUAD + (here_ref[1] ^ rel)
            row = pl.multiple_of(home * rows, rows)
            for k in range(groups):
                column = pl.multiple_of(lax.rem(here_ref[2] + (groups - k), groups) * columns, columns)
                out_ref[pl.ds(row, rows), pl.ds(column, columns)] = sources[rel][
                    base + d * rows : base + (d + 1) * rows, k * columns : (k + 1) * columns
                ]


def assemble(here, mine, over_y, rest, planes, groups):
    span, width = mine.shape
    vmem = pl.BlockSpec(memory_space=pltpu.VMEM)
    return pl.pallas_call(
        functools.partial(assemble_kernel, planes, groups),
        out_shape=jax.ShapeDtypeStruct((span * QUAD, width), mine.dtype),
        in_specs=[pl.BlockSpec(memory_space=pltpu.SMEM), vmem, vmem, vmem],
        out_specs=vmem,
        cost_estimate=SMALL,
        compiler_params=pltpu.CompilerParams(vmem_limit_bytes=32 << 20),
        name="assemble",
    )(here, mine, over_y, rest)


def after(array, *others):
    return lax.optimization_barrier((array, *others))[0]


def shards(tokens, out_grad, routes, route_weight, example_ids, in_proj, out_proj, queries):
    token_count, model_width = tokens.shape
    owned = in_proj.shape[0]
    n, groups = lax.axis_size("expert"), lax.axis_size("groups")
    planes = n // QUAD
    me, group = lax.axis_index("expert"), lax.axis_index("groups")
    plane, spot = me // QUAD, me % QUAD

    def move(array, hops):
        pairs = [(a * QUAD + q, b * QUAD + q) for a, b in hops for q in range(QUAD)]
        return lax.ppermute(array, "expert", pairs)

    def swap(array, bit):
        return lax.ppermute(array, "expert", [(i, i ^ bit) for i in range(n)])

    weights = jnp.swapaxes(in_proj, 1, 2).reshape(owned * RANK, model_width)
    half = weights.shape[0] // 2

    width = queries.shape[1] // groups
    lined = lax.dynamic_slice_in_dim(queries, group * width, width, axis=1)
    lined = jnp.concatenate([lined, swap(lined, QUAD)], axis=0)
    first = after(tokens, lined)
    over_core = swap(weights, 1)
    bit = 2 * QUAD
    while bit < n:
        lined = jnp.concatenate([lined, swap(lined, bit)], axis=0)
        bit *= 2

    ways_home = []
    for s in range(1, planes):
        up_home = [(p, p - s) for p in range(s, planes)]
        down_home = [(p, p + s) for p in range(planes - s)]
        ways_home.extend([up_home + down_home] if 2 * s >= planes else [up_home, down_home])

    homes = []
    for home in ways_home:
        back = -jnp.ones((), jnp.int32)
        for a, b in home:
            back = jnp.where(plane == b, a, back)
        homes.append(back)
    grad_side = jnp.dot(out_grad, out_proj, preferred_element_type=jnp.float32)
    rel = jnp.arange(QUAD, dtype=jnp.int32)
    inner = ((spot ^ rel)[:, None] * owned + jnp.arange(owned, dtype=jnp.int32)[None, :]).reshape(-1)
    place = jnp.stack([plane] + homes)
    expert_ids = jnp.where(place[:, None] >= 0, place[:, None] * (QUAD * owned) + inner[None, :], -1).reshape(-1)
    gate = jnp.sum(
        jnp.where(routes.T[None, :, :] == expert_ids[:, None, None], route_weight.T[None, :, :], 0.0), axis=1
    )
    local_ids = example_ids.reshape(token_count)
    member = local_ids[:, None] == jnp.arange(EX_DEV, dtype=jnp.int32)[None, :]
    counts = jnp.sum(member.astype(jnp.float32), axis=0)
    counts = jnp.broadcast_to(counts[:, None], (EX_DEV, RANK))
    repeated = jnp.concatenate([grad_side] * EX_DEV, axis=1)
    widely = jnp.repeat(member, RANK, axis=1)
    wide = jnp.where(
        widely[None], (gate[:, :, None] * repeated[None]).astype(jnp.bfloat16), jnp.zeros((), jnp.bfloat16)
    )

    over_y = swap(weights[:half], 2)
    up, down = first, first
    arrived, steps = [], []
    for s in range(1, planes):
        up_hops = [(p, p + 1) for p in range(s - 1, planes - 1)]
        down_hops = [(p, p - 1) for p in range(1, planes - s + 1)]
        if s == 2:
            up, down = after(up, lined, wide), after(down, lined, wide)
            ranged = [lined] + [
                lax.ppermute(after(lined, over_y, up, down), "groups", [(g, (g + k) % groups) for g in range(groups)])
                for k in range(1, groups)
            ]
        elif s == 3:
            up, down = after(up, *ranged), after(down, *ranged)
        if 2 * s > planes + 1:
            up = down = move(up, up_hops + down_hops)
        else:
            up, down = move(up, up_hops), move(down, down_hops)
            if 2 * s >= planes:
                up = down = up + down
        steps.append(up)
        arrived.extend([up] if 2 * s >= planes else [up, down])

    over_y_late = swap(after(weights[half:], arrived[0]), 2)
    over_y_all = jnp.concatenate([over_y, over_y_late], axis=0)
    across = swap(after(over_y_all, steps[1]), 1)
    quad_weights = [weights, over_core, over_y_all, across]

    experts = QUAD * owned
    own, *sides = project([tokens] + arrived[:-1], quad_weights)
    returned = [move(side, home) for side, home in zip(sides, ways_home[:-1])]
    mine = after(jnp.concatenate(ranged, axis=1), over_y_all, steps[1])
    mine_over_y = swap(mine, 2)
    side = project([after(arrived[-1], *returned)], quad_weights)[0]
    late = move(side, ways_home[-1])
    early = combine([own] + returned, wide[:-experts])
    rest = swap(after(jnp.concatenate([mine, mine_over_y], axis=0), side), 1)
    here = jnp.stack([plane, spot, group]).astype(jnp.int32)
    all_queries = assemble(here, mine, mine_over_y, rest, planes, groups)
    sketches = combine([late], wide[-experts:], early, counts)
    sketches = sketches.reshape(EX_DEV, RANK * RANK)
    scores = lax.dot_general(sketches.astype(jnp.bfloat16), all_queries, NT, preferred_element_type=jnp.float32)
    return (sketches, scores)


def solution(mesh):
    placed = (
        P(("groups", "expert"), None),
        P(("groups", "expert"), None),
        P(("groups", "expert"), None),
        P(("groups", "expert"), None),
        P(("groups", "expert"), None),
        P("expert", None, None),
        P(),
        P("expert", None),
    )
    return jax.shard_map(
        shards,
        mesh=mesh,
        in_specs=placed,
        out_specs=(P(("groups", "expert"), None), P(("groups", "expert"), None)),
        check_vma=False,
    )
```

```python
import functools

import jax
import jax.numpy as jnp
from jax import lax
from jax.experimental import pallas as pl
from jax.experimental.pallas import tpu as pltpu
from jax.sharding import PartitionSpec as P

RANK = 64
EX_DEV = 4
QUAD = 4
SLAB = 16

SMALL = pl.CostEstimate(flops=1024, bytes_accessed=1024, transcendentals=0)

NT = (((1,), (1,)), ((), ()))
TN = (((0,), (0,)), ((), ()))


def combine_kernel(blocks, experts, first, last, *refs):
    sides, wide = refs[:blocks], refs[blocks]
    total = jnp.zeros((RANK, EX_DEV * RANK), jnp.float32) if first else refs[blocks + 1][...]
    out = refs[-1]
    span = experts * RANK
    for b in range(blocks):
        slabs = [sides[b][:, g * span : (g + 1) * span] for g in range(wide.shape[1] // SLAB)]
        side = jnp.concatenate(slabs, axis=0)
        for e in range(experts):
            total += lax.dot_general(
                side[:, e * RANK : (e + 1) * RANK],
                wide[b * experts + e],
                TN,
                preferred_element_type=jnp.float32,
            )
    if last:
        counts = refs[-2]
        for x in range(EX_DEV):
            out[x] = total[:, x * RANK : (x + 1) * RANK] / counts[x : x + 1, :]
    else:
        out[...] = total


def combine(sides, wide, total=None, counts=None):
    experts = wide.shape[0] // len(sides)
    extra = [a for a in (total, counts) if a is not None]
    shape = (RANK, EX_DEV * RANK) if counts is None else (EX_DEV, RANK, RANK)
    return pl.pallas_call(
        functools.partial(combine_kernel, len(sides), experts, total is None, counts is not None),
        out_shape=jax.ShapeDtypeStruct(shape, jnp.float32),
        in_specs=[pl.BlockSpec(memory_space=pltpu.VMEM)] * (len(sides) + 1 + len(extra)),
        out_specs=pl.BlockSpec(memory_space=pltpu.VMEM),
        cost_estimate=SMALL,
        compiler_params=pltpu.CompilerParams(vmem_limit_bytes=32 << 20),
        name="combine",
    )(*sides, wide, *extra)


def project_kernel(blocks, rows, *refs):
    parts, weights = refs[:blocks], refs[blocks : blocks + QUAD]
    outs, total = refs[blocks + QUAD : -1], refs[-1]
    depth = 1024
    total[...] = jnp.zeros_like(total)

    @pl.loop(0, parts[0].shape[1] // depth)
    def _(i):
        span = pl.ds(pl.multiple_of(i * depth, depth), depth)
        left = jnp.concatenate([p[:rows, span] for p in parts], axis=0)
        right = jnp.concatenate([w[:, span] for w in weights], axis=0)
        total[...] += lax.dot_general(left, right, NT, preferred_element_type=jnp.float32)

    width = total.shape[1]
    for b in range(blocks):
        for g in range(rows // SLAB):
            top = b * rows + g * SLAB
            outs[b][:, g * width : (g + 1) * width] = total[top : top + SLAB].astype(jnp.bfloat16)
        used = rows // SLAB * width
        if outs[b].shape[1] > used:
            outs[b][:, used:] = parts[-1][rows:, :]


def project(parts, rows, weights, riders=()):
    width = QUAD * weights[0].shape[0]
    vmem = pl.BlockSpec(memory_space=pltpu.VMEM)
    sizes = [rows // SLAB * width + (parts[-1].shape[1] if b in riders else 0) for b in range(len(parts))]
    return pl.pallas_call(
        functools.partial(project_kernel, len(parts), rows),
        out_shape=[jax.ShapeDtypeStruct((SLAB, size), jnp.bfloat16) for size in sizes],
        in_specs=[vmem] * (len(parts) + QUAD),
        out_specs=[vmem] * len(parts),
        scratch_shapes=[pltpu.VMEM((rows * len(parts), width), jnp.float32)],
        cost_estimate=SMALL,
        compiler_params=pltpu.CompilerParams(vmem_limit_bytes=40 << 20),
        name="project",
    )(*parts, *weights)


def assemble_kernel(blocks, where_ref, held_ref, late_ref, over_y_ref, late_over_y_ref, across_ref, out_ref):
    rows = late_ref.shape[0]
    span = blocks * rows
    sources = (
        ((held_ref, 0), (late_ref, 0)),
        ((across_ref, 0), (across_ref, 2 * span)),
        ((over_y_ref, 0), (late_over_y_ref, 0)),
        ((across_ref, span), (across_ref, 2 * span + rows)),
    )
    for b in range(blocks + 1):

        @pl.when(where_ref[b] >= 0)
        def _():
            for rel in range(QUAD):
                source, base = sources[rel][b // blocks]
                top = base + b % blocks * rows
                home = where_ref[b] * QUAD + (where_ref[blocks + 1] ^ rel)
                out_ref[pl.ds(pl.multiple_of(home * rows, rows), rows), :] = source[top : top + rows, :]


def assemble(where, total, *held):
    vmem = pl.BlockSpec(memory_space=pltpu.VMEM)
    return pl.pallas_call(
        functools.partial(assemble_kernel, where.shape[0] - 2),
        out_shape=jax.ShapeDtypeStruct((total, held[0].shape[1]), held[0].dtype),
        in_specs=[pl.BlockSpec(memory_space=pltpu.SMEM)] + [vmem] * len(held),
        out_specs=vmem,
        cost_estimate=SMALL,
        compiler_params=pltpu.CompilerParams(vmem_limit_bytes=40 << 20),
        name="assemble",
    )(where, *held)


def after(array, *others):
    return lax.optimization_barrier((array, *others))[0]


def shards(tokens, out_grad, routes, route_weight, example_ids, in_proj, out_proj, queries):
    token_count, model_width = tokens.shape
    owned = in_proj.shape[0]
    n = lax.axis_size("expert")
    planes = n // QUAD
    me = lax.axis_index("expert")
    plane, spot = me // QUAD, me % QUAD

    def move(array, hops):
        pairs = [(a * QUAD + q, b * QUAD + q) for a, b in hops for q in range(QUAD)]
        return lax.ppermute(array, "expert", pairs)

    def swap(array, bit):
        return lax.ppermute(array, "expert", [(i, i ^ bit) for i in range(n)])

    weights = jnp.swapaxes(in_proj, 1, 2).reshape(owned * RANK, model_width)

    origins, ways_home = [plane], []
    for s in range(1, planes):
        up_home = [(p, p - s) for p in range(s, planes)]
        down_home = [(p, p + s) for p in range(planes - s)]
        from_up = jnp.where(plane >= s, plane - s, -1)
        from_down = jnp.where(plane + s < planes, plane + s, -1)
        if 2 * s >= planes:
            origins.append(jnp.maximum(from_up, from_down))
            ways_home.append(up_home + down_home)
        else:
            origins.extend([from_up, from_down])
            ways_home.extend([up_home, down_home])

    homes = []
    for home in ways_home:
        back = -jnp.ones((), jnp.int32)
        for a, b in home:
            back = jnp.where(plane == b, a, back)
        homes.append(back)
    grad_side = jnp.dot(out_grad, out_proj, preferred_element_type=jnp.float32)
    rel = jnp.arange(QUAD, dtype=jnp.int32)
    inner = ((spot ^ rel)[:, None] * owned + jnp.arange(owned, dtype=jnp.int32)[None, :]).reshape(-1)
    place = jnp.stack([plane] + homes)
    expert_ids = jnp.where(place[:, None] >= 0, place[:, None] * (QUAD * owned) + inner[None, :], -1).reshape(-1)
    gate = jnp.sum(
        jnp.where(routes.T[None, :, :] == expert_ids[:, None, None], route_weight.T[None, :, :], 0.0), axis=1
    )
    local_ids = example_ids.reshape(token_count)
    member = local_ids[:, None] == jnp.arange(EX_DEV, dtype=jnp.int32)[None, :]
    counts = jnp.sum(member.astype(jnp.float32), axis=0)
    counts = jnp.broadcast_to(counts[:, None], (EX_DEV, RANK))
    repeated = jnp.concatenate([grad_side] * EX_DEV, axis=1)
    widely = jnp.repeat(member, RANK, axis=1)
    wide = jnp.where(
        widely[None], (gate[:, :, None] * repeated[None]).astype(jnp.bfloat16), jnp.zeros((), jnp.bfloat16)
    )

    mine = jnp.concatenate([tokens, queries], axis=0)
    up, down = mine, mine
    arrived = []
    for s in range(1, planes):
        up_hops = [(p, p + 1) for p in range(s - 1, planes - 1)]
        down_hops = [(p, p - 1) for p in range(1, planes - s + 1)]
        if s == 2:
            up, down = after(up, wide), after(down, wide)
        if s == planes - 1:
            up, down = up[:token_count], down[:token_count]
        if 2 * s > planes + 1:
            up = down = move(up, up_hops + down_hops)
        else:
            up, down = move(up, up_hops), move(down, down_hops)
            if 2 * s >= planes:
                up = down = up + down
        arrived.extend([up] if 2 * s >= planes else [up, down])
    last = arrived.pop()

    over_core = swap(weights, 1)
    over_y = swap(weights, 2)
    across = swap(after(over_y, arrived[-1]), 1)
    quad_weights = [weights, over_core, over_y, across]

    experts = QUAD * owned
    own, *sides = project([tokens] + arrived, token_count, quad_weights, riders=(1, 2))
    returned = [move(side, home) for side, home in zip(sides, ways_home)]
    side = project([after(last, *returned)], token_count, quad_weights)[0]
    late = move(side, ways_home[-1])
    early = combine([own] + returned, wide[:-experts])

    held = jnp.concatenate([after(queries, arrived[0])] + [block[token_count:] for block in arrived], axis=0)
    held_late = jnp.where(plane == 0, returned[0][:, own.shape[1] :], returned[1][:, own.shape[1] :])
    over_y = swap(held, 2)
    late_over_y = swap(held_late, 2)
    across = swap(jnp.concatenate(after((held, over_y, held_late, late_over_y), side), axis=0), 1)
    where = jnp.stack(origins + [spot]).astype(jnp.int32)
    all_queries = assemble(where, n * queries.shape[0], held, held_late, over_y, late_over_y, across)
    sketches = combine([late], wide[-experts:], early, counts)
    sketches = sketches.reshape(EX_DEV, RANK * RANK)
    scores = lax.dot_general(sketches.astype(jnp.bfloat16), all_queries, NT, preferred_element_type=jnp.float32)
    return (sketches, scores)


def solution(mesh):
    placed = (
        P(("groups", "expert"), None),
        P(("groups", "expert"), None),
        P(("groups", "expert"), None),
        P(("groups", "expert"), None),
        P(("groups", "expert"), None),
        P("expert", None, None),
        P(),
        P("expert", None),
    )
    return jax.shard_map(
        shards,
        mesh=mesh,
        in_specs=placed,
        out_specs=(P(("groups", "expert"), None), P(("groups", "expert"), None)),
        check_vma=False,
    )
```

```python
import functools
import math

import jax
import jax.numpy as jnp
from jax import lax
from jax.experimental import pallas as pl
from jax.experimental.pallas import tpu as pltpu
from jax.sharding import PartitionSpec as P

RANK = 64
EX_DEV = 4
QUAD = 4
SLAB = 16

SMALL = pl.CostEstimate(flops=1024, bytes_accessed=1024, transcendentals=0)

NT = (((1,), (1,)), ((), ()))
TN = (((0,), (0,)), ((), ()))


def room(*arrays):
    return sum(math.prod(a.shape) * jnp.dtype(a.dtype).itemsize for a in arrays) + (6 << 20)


def combine_kernel(blocks, experts, first, last, *refs):
    sides, wide = refs[:blocks], refs[blocks]
    total = jnp.zeros((RANK, EX_DEV * RANK), jnp.float32) if first else refs[blocks + 1][...]
    out = refs[-1]
    span = experts * RANK
    for b in range(blocks):
        slabs = [sides[b][:, g * span : (g + 1) * span] for g in range(wide.shape[1] // SLAB)]
        side = jnp.concatenate(slabs, axis=0)
        for e in range(experts):
            total += lax.dot_general(
                side[:, e * RANK : (e + 1) * RANK],
                wide[b * experts + e],
                TN,
                preferred_element_type=jnp.float32,
            )
    if last:
        counts = refs[-2]
        for x in range(EX_DEV):
            out[x] = total[:, x * RANK : (x + 1) * RANK] / counts[x : x + 1, :]
    else:
        out[...] = total


def combine(sides, wide, total=None, counts=None):
    experts = wide.shape[0] // len(sides)
    extra = [a for a in (total, counts) if a is not None]
    shape = (RANK, EX_DEV * RANK) if counts is None else (EX_DEV, RANK, RANK)
    return pl.pallas_call(
        functools.partial(combine_kernel, len(sides), experts, total is None, counts is not None),
        out_shape=jax.ShapeDtypeStruct(shape, jnp.float32),
        in_specs=[pl.BlockSpec(memory_space=pltpu.VMEM)] * (len(sides) + 1 + len(extra)),
        out_specs=pl.BlockSpec(memory_space=pltpu.VMEM),
        cost_estimate=SMALL,
        compiler_params=pltpu.CompilerParams(vmem_limit_bytes=room(*sides, wide)),
        name="combine",
    )(*sides, wide, *extra)


def project_kernel(blocks, rows, *refs):
    parts, weights = refs[:blocks], refs[blocks : blocks + QUAD]
    outs, total = refs[blocks + QUAD : -1], refs[-1]
    depth = 1024
    total[...] = jnp.zeros_like(total)

    @pl.loop(0, parts[0].shape[1] // depth)
    def _(i):
        span = pl.ds(pl.multiple_of(i * depth, depth), depth)
        left = jnp.concatenate([p[:rows, span] for p in parts], axis=0)
        right = jnp.concatenate([w[:, span] for w in weights], axis=0)
        total[...] += lax.dot_general(left, right, NT, preferred_element_type=jnp.float32)

    width = total.shape[1]
    for b in range(blocks):
        for g in range(rows // SLAB):
            top = b * rows + g * SLAB
            outs[b][:, g * width : (g + 1) * width] = total[top : top + SLAB].astype(jnp.bfloat16)


def project(parts, rows, weights):
    width = QUAD * weights[0].shape[0]
    vmem = pl.BlockSpec(memory_space=pltpu.VMEM)
    total = jax.ShapeDtypeStruct((rows * len(parts), width), jnp.float32)
    return pl.pallas_call(
        functools.partial(project_kernel, len(parts), rows),
        out_shape=[jax.ShapeDtypeStruct((SLAB, rows // SLAB * width), jnp.bfloat16)] * len(parts),
        in_specs=[vmem] * (len(parts) + QUAD),
        out_specs=[vmem] * len(parts),
        scratch_shapes=[pltpu.VMEM(total.shape, total.dtype)],
        cost_estimate=SMALL,
        compiler_params=pltpu.CompilerParams(vmem_limit_bytes=room(*parts, *weights, total, total)),
        name="project",
    )(*parts, *weights)


def assemble_kernel(early, blocks, rows, where_ref, *refs):
    out_ref = refs[-1]
    for b in range(blocks):
        late, at, length = (3, b - early, blocks - early) if b >= early else (0, b, early)
        mine_ref, over_y_ref, across_ref = refs[late : late + 3]
        sources = ((mine_ref, at), (across_ref, at), (over_y_ref, at), (across_ref, length + at))

        @pl.when(where_ref[b] >= 0)
        def _():
            for rel in range(QUAD):
                source, at = sources[rel]
                home = where_ref[b] * QUAD + (where_ref[blocks] ^ rel)
                out_ref[pl.ds(pl.multiple_of(home * rows, rows), rows), :] = source[at * rows : (at + 1) * rows, :]


def assemble(where, total, rows, *held):
    vmem = pl.BlockSpec(memory_space=pltpu.VMEM)
    out = jax.ShapeDtypeStruct((total, held[0].shape[1]), held[0].dtype)
    return pl.pallas_call(
        functools.partial(assemble_kernel, held[0].shape[0] // rows, where.shape[0] - 1, rows),
        out_shape=out,
        in_specs=[pl.BlockSpec(memory_space=pltpu.SMEM)] + [vmem] * len(held),
        out_specs=vmem,
        cost_estimate=SMALL,
        compiler_params=pltpu.CompilerParams(vmem_limit_bytes=room(out, *held)),
        name="assemble",
    )(where, *held)


def after(array, *others):
    return lax.optimization_barrier((array, *others))[0]


def shards(tokens, out_grad, routes, route_weight, example_ids, in_proj, out_proj, queries):
    token_count, model_width = tokens.shape
    owned = in_proj.shape[0]
    n = lax.axis_size("expert")
    planes = n // QUAD
    me = lax.axis_index("expert")
    plane, spot = me // QUAD, me % QUAD

    def move(array, hops):
        pairs = [(a * QUAD + q, b * QUAD + q) for a, b in hops for q in range(QUAD)]
        return lax.ppermute(array, "expert", pairs)

    def swap(array, bit):
        return lax.ppermute(array, "expert", [(i, i ^ bit) for i in range(n)])

    weights = jnp.swapaxes(in_proj, 1, 2).reshape(owned * RANK, model_width)

    origins, ways_home = [plane], []
    for s in range(1, planes):
        up_home = [(p, p - s) for p in range(s, planes)]
        down_home = [(p, p + s) for p in range(planes - s)]
        from_up = jnp.where(plane >= s, plane - s, -1)
        from_down = jnp.where(plane + s < planes, plane + s, -1)
        if 2 * s >= planes:
            origins.append(jnp.maximum(from_up, from_down))
            ways_home.append(up_home + down_home)
        else:
            origins.extend([from_up, from_down])
            ways_home.extend([up_home, down_home])

    homes = []
    for home in ways_home:
        back = -jnp.ones((), jnp.int32)
        for a, b in home:
            back = jnp.where(plane == b, a, back)
        homes.append(back)
    grad_side = jnp.dot(out_grad, out_proj, preferred_element_type=jnp.float32)
    rel = jnp.arange(QUAD, dtype=jnp.int32)
    inner = ((spot ^ rel)[:, None] * owned + jnp.arange(owned, dtype=jnp.int32)[None, :]).reshape(-1)
    place = jnp.stack([plane] + homes)
    expert_ids = jnp.where(place[:, None] >= 0, place[:, None] * (QUAD * owned) + inner[None, :], -1).reshape(-1)
    gate = jnp.sum(
        jnp.where(routes.T[None, :, :] == expert_ids[:, None, None], route_weight.T[None, :, :], 0.0), axis=1
    )
    local_ids = example_ids.reshape(token_count)
    member = local_ids[:, None] == jnp.arange(EX_DEV, dtype=jnp.int32)[None, :]
    counts = jnp.sum(member.astype(jnp.float32), axis=0)
    counts = jnp.broadcast_to(counts[:, None], (EX_DEV, RANK))
    repeated = jnp.concatenate([grad_side] * EX_DEV, axis=1)
    widely = jnp.repeat(member, RANK, axis=1)
    wide = jnp.where(
        widely[None], (gate[:, :, None] * repeated[None]).astype(jnp.bfloat16), jnp.zeros((), jnp.bfloat16)
    )

    over_core = swap(weights, 1)
    over_y = swap(weights, 2)

    middle = (planes + 1) // 2
    experts = QUAD * owned
    mine = jnp.concatenate([tokens, queries], axis=0)
    up, down = mine, mine
    first = []
    for s in range(1, middle):
        if s > 1:
            up, down = after(up, wide), after(down, wide)
        up, down = move(up, [(p, p + 1) for p in range(s - 1, planes - 1)]), move(
            down, [(p, p - 1) for p in range(1, planes - s + 1)]
        )
        first.extend([up, down])
    across = swap(after(over_y, *first), 1)
    quad_weights = [weights, over_core, over_y, across]
    own, *sides = project([tokens] + first, token_count, quad_weights)
    returned = [move(side, home) for side, home in zip(sides, ways_home)]
    held = jnp.concatenate([queries] + [block[token_count:] for block in first], axis=0)
    held_over_y = swap(held, 2)

    rider = jnp.where(plane == middle, down[token_count:], up[token_count:])
    up, down = after(up, wide), after(down, wide)
    held_late = []
    for s in range(middle, planes):
        up_hops = [(p, p + 1) for p in range(s - 1, planes - 1)]
        down_hops = [(p, p - 1) for p in range(1, planes - s + 1)]
        if s == planes - 1:
            up = down = up[:token_count]
        if s == middle:
            up, down = move(up, up_hops), move(down, down_hops)
            up = down = up + after(down, held_over_y, *sides)
        else:
            up = down = move(up, up_hops + down_hops)
        if s == middle:
            held_across = swap(jnp.concatenate(after((held, held_over_y), up), axis=0), 1)
        wait = returned if s == planes - 1 else [held_across]
        (side,) = project([after(up, *wait)], token_count, quad_weights)
        if s == middle:
            side = jnp.concatenate([side, rider], axis=1)
        returned.append(move(side, ways_home[len(returned)]))
        if s == middle:
            rider = returned[-1][:, own.shape[1] :]
        if s < planes - 1:
            held_late.append(up[token_count:])
    late = returned.pop()
    early = combine([own] + returned, wide[:-experts])

    held_late = after(jnp.concatenate(held_late + [rider], axis=0), side)
    late_over_y = swap(held_late, 2)
    late_across = swap(after(jnp.concatenate([held_late, late_over_y], axis=0), late), 1)
    spread = (held, held_over_y, held_across, held_late, late_over_y, late_across)
    where = jnp.stack(origins + [spot]).astype(jnp.int32)
    all_queries = assemble(where, n * queries.shape[0], queries.shape[0], *spread)
    sketches = combine([late], wide[-experts:], early, counts)
    sketches = sketches.reshape(EX_DEV, RANK * RANK)
    scores = lax.dot_general(sketches.astype(jnp.bfloat16), all_queries, NT, preferred_element_type=jnp.float32)
    return (sketches, scores)


def solution(mesh):
    placed = (
        P(("groups", "expert"), None),
        P(("groups", "expert"), None),
        P(("groups", "expert"), None),
        P(("groups", "expert"), None),
        P(("groups", "expert"), None),
        P("expert", None, None),
        P(),
        P("expert", None),
    )
    return jax.shard_map(
        shards,
        mesh=mesh,
        in_specs=placed,
        out_specs=(P(("groups", "expert"), None), P(("groups", "expert"), None)),
        check_vma=False,
    )
```

```python
import functools
import math

import jax
import jax.numpy as jnp
from jax import lax
from jax.experimental import pallas as pl
from jax.experimental.pallas import tpu as pltpu
from jax.sharding import PartitionSpec as P

RANK = 64
EX_DEV = 4
QUAD = 4
SLAB = 16

SMALL = pl.CostEstimate(flops=1024, bytes_accessed=1024, transcendentals=0)

NT = (((1,), (1,)), ((), ()))
TN = (((0,), (0,)), ((), ()))


def room(*arrays):
    return sum(math.prod(a.shape) * jnp.dtype(a.dtype).itemsize for a in arrays) + (6 << 20)


def combine_kernel(blocks, experts, first, last, *refs):
    sides, wide = refs[:blocks], refs[blocks]
    total = jnp.zeros((RANK, EX_DEV * RANK), jnp.float32) if first else refs[blocks + 1][...]
    out = refs[-1]
    span = experts * RANK
    for b in range(blocks):
        slabs = [sides[b][:, g * span : (g + 1) * span] for g in range(wide.shape[1] // SLAB)]
        side = jnp.concatenate(slabs, axis=0)
        for e in range(experts):
            total += lax.dot_general(
                side[:, e * RANK : (e + 1) * RANK],
                wide[b * experts + e],
                TN,
                preferred_element_type=jnp.float32,
            )
    if last:
        counts = refs[-2]
        for x in range(EX_DEV):
            out[x] = total[:, x * RANK : (x + 1) * RANK] / counts[x : x + 1, :]
    else:
        out[...] = total


def combine(sides, wide, total=None, counts=None):
    experts = wide.shape[0] // len(sides)
    extra = [a for a in (total, counts) if a is not None]
    shape = (RANK, EX_DEV * RANK) if counts is None else (EX_DEV, RANK, RANK)
    return pl.pallas_call(
        functools.partial(combine_kernel, len(sides), experts, total is None, counts is not None),
        out_shape=jax.ShapeDtypeStruct(shape, jnp.float32),
        in_specs=[pl.BlockSpec(memory_space=pltpu.VMEM)] * (len(sides) + 1 + len(extra)),
        out_specs=pl.BlockSpec(memory_space=pltpu.VMEM),
        cost_estimate=SMALL,
        compiler_params=pltpu.CompilerParams(vmem_limit_bytes=room(*sides, wide)),
        name="combine",
    )(*sides, wide, *extra)


def project_kernel(blocks, rows, *refs):
    parts, weights = refs[:blocks], refs[blocks : blocks + QUAD]
    outs, total = refs[blocks + QUAD : -1], refs[-1]
    depth = 1024
    total[...] = jnp.zeros_like(total)

    @pl.loop(0, parts[0].shape[1] // depth)
    def _(i):
        span = pl.ds(pl.multiple_of(i * depth, depth), depth)
        left = jnp.concatenate([p[:rows, span] for p in parts], axis=0)
        right = jnp.concatenate([w[:, span] for w in weights], axis=0)
        total[...] += lax.dot_general(left, right, NT, preferred_element_type=jnp.float32)

    width = total.shape[1]
    for b in range(blocks):
        for g in range(rows // SLAB):
            top = b * rows + g * SLAB
            outs[b][:, g * width : (g + 1) * width] = total[top : top + SLAB].astype(jnp.bfloat16)


def project(parts, rows, weights):
    width = QUAD * weights[0].shape[0]
    vmem = pl.BlockSpec(memory_space=pltpu.VMEM)
    total = jax.ShapeDtypeStruct((rows * len(parts), width), jnp.float32)
    return pl.pallas_call(
        functools.partial(project_kernel, len(parts), rows),
        out_shape=[jax.ShapeDtypeStruct((SLAB, rows // SLAB * width), jnp.bfloat16)] * len(parts),
        in_specs=[vmem] * (len(parts) + QUAD),
        out_specs=[vmem] * len(parts),
        scratch_shapes=[pltpu.VMEM(total.shape, total.dtype)],
        cost_estimate=SMALL,
        compiler_params=pltpu.CompilerParams(vmem_limit_bytes=room(*parts, *weights, total, total)),
        name="project",
    )(*parts, *weights)


def assemble_kernel(planes, groups, here_ref, mine_ref, over_y_ref, rest_ref, out_ref):
    span = mine_ref.shape[0]
    rows, columns = span // planes, out_ref.shape[1] // groups
    sources = (mine_ref, rest_ref, over_y_ref, rest_ref)
    for rel in range(QUAD):
        base = span if rel == 3 else 0
        for d in range(planes):
            home = (here_ref[0] ^ d) * QUAD + (here_ref[1] ^ rel)
            row = pl.multiple_of(home * rows, rows)
            for k in range(groups):
                column = pl.multiple_of(lax.rem(here_ref[2] + (groups - k), groups) * columns, columns)
                out_ref[pl.ds(row, rows), pl.ds(column, columns)] = sources[rel][
                    base + d * rows : base + (d + 1) * rows, k * columns : (k + 1) * columns
                ]


def assemble(here, mine, over_y, rest, planes, groups):
    span, width = mine.shape
    vmem = pl.BlockSpec(memory_space=pltpu.VMEM)
    return pl.pallas_call(
        functools.partial(assemble_kernel, planes, groups),
        out_shape=jax.ShapeDtypeStruct((span * QUAD, width), mine.dtype),
        in_specs=[pl.BlockSpec(memory_space=pltpu.SMEM), vmem, vmem, vmem],
        out_specs=vmem,
        cost_estimate=SMALL,
        compiler_params=pltpu.CompilerParams(vmem_limit_bytes=room(mine, mine, mine, mine, mine, over_y, rest)),
        name="assemble",
    )(here, mine, over_y, rest)


def after(array, *others):
    return lax.optimization_barrier((array, *others))[0]


def shards(tokens, out_grad, routes, route_weight, example_ids, in_proj, out_proj, queries):
    token_count, model_width = tokens.shape
    owned = in_proj.shape[0]
    n, groups = lax.axis_size("expert"), lax.axis_size("groups")
    planes = n // QUAD
    me, group = lax.axis_index("expert"), lax.axis_index("groups")
    plane, spot = me // QUAD, me % QUAD

    def move(array, hops):
        pairs = [(a * QUAD + q, b * QUAD + q) for a, b in hops for q in range(QUAD)]
        return lax.ppermute(array, "expert", pairs)

    def swap(array, bit):
        return lax.ppermute(array, "expert", [(i, i ^ bit) for i in range(n)])

    weights = jnp.swapaxes(in_proj, 1, 2).reshape(owned * RANK, model_width)

    ways_home = []
    for s in range(1, planes):
        up_home = [(p, p - s) for p in range(s, planes)]
        down_home = [(p, p + s) for p in range(planes - s)]
        ways_home.extend([up_home + down_home] if 2 * s >= planes else [up_home, down_home])

    homes = []
    for home in ways_home:
        back = -jnp.ones((), jnp.int32)
        for a, b in home:
            back = jnp.where(plane == b, a, back)
        homes.append(back)
    grad_side = jnp.dot(out_grad, out_proj, preferred_element_type=jnp.float32)
    rel = jnp.arange(QUAD, dtype=jnp.int32)
    inner = ((spot ^ rel)[:, None] * owned + jnp.arange(owned, dtype=jnp.int32)[None, :]).reshape(-1)
    place = jnp.stack([plane] + homes)
    expert_ids = jnp.where(place[:, None] >= 0, place[:, None] * (QUAD * owned) + inner[None, :], -1).reshape(-1)
    gate = jnp.sum(
        jnp.where(routes.T[None, :, :] == expert_ids[:, None, None], route_weight.T[None, :, :], 0.0), axis=1
    )
    local_ids = example_ids.reshape(token_count)
    member = local_ids[:, None] == jnp.arange(EX_DEV, dtype=jnp.int32)[None, :]
    counts = jnp.sum(member.astype(jnp.float32), axis=0)
    counts = jnp.broadcast_to(counts[:, None], (EX_DEV, RANK))
    repeated = jnp.concatenate([grad_side] * EX_DEV, axis=1)
    widely = jnp.repeat(member, RANK, axis=1)
    experts = QUAD * owned

    def widen(part):
        spread = (part[:, :, None] * repeated[None]).astype(jnp.bfloat16)
        return jnp.where(widely[None], spread, jnp.zeros((), jnp.bfloat16))

    wide, wide_late = widen(gate[:-experts]), widen(gate[-experts:])

    over_y = swap(weights, 2)

    width = queries.shape[1] // groups
    lined = lax.dynamic_slice_in_dim(queries, group * width, width, axis=1)
    lined = jnp.concatenate([lined, swap(lined, QUAD)], axis=0)

    middle = (planes + 1) // 2
    up, down = tokens, tokens
    first = []
    for s in range(1, middle):
        up, down = move(up, [(p, p + 1) for p in range(s - 1, planes - 1)]), move(
            down, [(p, p - 1) for p in range(1, planes - s + 1)]
        )
        first.extend([up, down])
    over_core = swap(weights, 1)
    lined = after(lined, wide, wide_late, *first)
    bit = 2 * QUAD
    while bit < n:
        lined = jnp.concatenate([lined, swap(lined, bit)], axis=0)
        bit *= 2

    for s in range(middle, planes):
        up_hops = [(p, p + 1) for p in range(s - 1, planes - 1)]
        down_hops = [(p, p - 1) for p in range(1, planes - s + 1)]
        if s == middle:
            up, down = move(up, up_hops), move(down, down_hops)
            up = down = up + down
            across = swap(after(over_y, up), 1)
            quad_weights = [weights, over_core, over_y, across]
            lined = after(lined, up)
            ranged = [lined] + [
                lax.ppermute(lined, "groups", [(g, (g + k) % groups) for g in range(groups)]) for k in range(1, groups)
            ]
            own, *sides = project([tokens] + first + [up], token_count, quad_weights)
            returned = [move(side, home) for side, home in zip(sides, ways_home)]
            mine = jnp.concatenate(ranged, axis=1)
            mine_over_y = swap(mine, 2)
        else:
            up = down = move(up, up_hops + down_hops)
            wait = returned if s == planes - 1 else []
            (side,) = project([after(up, *wait)], token_count, quad_weights)
            returned.append(move(side, ways_home[len(returned)]))
    late = returned.pop()
    early = combine([own] + returned, wide)

    rest = swap(after(jnp.concatenate([mine, mine_over_y], axis=0), late), 1)
    here = jnp.stack([plane, spot, group]).astype(jnp.int32)
    all_queries = assemble(here, mine, mine_over_y, rest, planes, groups)
    sketches = combine([late], wide_late, early, counts)
    sketches = sketches.reshape(EX_DEV, RANK * RANK)
    scores = lax.dot_general(sketches.astype(jnp.bfloat16), all_queries, NT, preferred_element_type=jnp.float32)
    return (sketches, scores)


def solution(mesh):
    placed = (
        P(("groups", "expert"), None),
        P(("groups", "expert"), None),
        P(("groups", "expert"), None),
        P(("groups", "expert"), None),
        P(("groups", "expert"), None),
        P("expert", None, None),
        P(),
        P("expert", None),
    )
    return jax.shard_map(
        shards,
        mesh=mesh,
        in_specs=placed,
        out_specs=(P(("groups", "expert"), None), P(("groups", "expert"), None)),
        check_vma=False,
    )
```

```python
import functools
import math

import jax
import jax.numpy as jnp
from jax import lax
from jax.experimental import pallas as pl
from jax.experimental.pallas import tpu as pltpu
from jax.sharding import PartitionSpec as P

RANK = 64
EX_DEV = 4
QUAD = 4
SLAB = 16

SMALL = pl.CostEstimate(flops=1024, bytes_accessed=1024, transcendentals=0)

NT = (((1,), (1,)), ((), ()))
TN = (((0,), (0,)), ((), ()))


def room(*arrays):
    return sum(math.prod(a.shape) * jnp.dtype(a.dtype).itemsize for a in arrays) + (6 << 20)


def combine_kernel(blocks, experts, first, last, *refs):
    sides, wide = refs[:blocks], refs[blocks]
    total = jnp.zeros((RANK, EX_DEV * RANK), jnp.float32) if first else refs[blocks + 1][...]
    out = refs[-1]
    span = experts * RANK
    for b in range(blocks):
        slabs = [sides[b][:, g * span : (g + 1) * span] for g in range(wide.shape[1] // SLAB)]
        side = jnp.concatenate(slabs, axis=0)
        for e in range(experts):
            total += lax.dot_general(
                side[:, e * RANK : (e + 1) * RANK],
                wide[b * experts + e],
                TN,
                preferred_element_type=jnp.float32,
            )
    if last:
        counts = refs[-2]
        for x in range(EX_DEV):
            out[x] = total[:, x * RANK : (x + 1) * RANK] / counts[x : x + 1, :]
    else:
        out[...] = total


def combine(sides, wide, total=None, counts=None):
    experts = wide.shape[0] // len(sides)
    extra = [a for a in (total, counts) if a is not None]
    shape = (RANK, EX_DEV * RANK) if counts is None else (EX_DEV, RANK, RANK)
    return pl.pallas_call(
        functools.partial(combine_kernel, len(sides), experts, total is None, counts is not None),
        out_shape=jax.ShapeDtypeStruct(shape, jnp.float32),
        in_specs=[pl.BlockSpec(memory_space=pltpu.VMEM)] * (len(sides) + 1 + len(extra)),
        out_specs=pl.BlockSpec(memory_space=pltpu.VMEM),
        cost_estimate=SMALL,
        compiler_params=pltpu.CompilerParams(vmem_limit_bytes=room(*sides, wide)),
        name="combine",
    )(*sides, wide, *extra)


def project_kernel(blocks, rows, *refs):
    parts, weights = refs[:blocks], refs[blocks : blocks + QUAD]
    outs, total = refs[blocks + QUAD : -1], refs[-1]
    depth = 1024
    total[...] = jnp.zeros_like(total)

    @pl.loop(0, parts[0].shape[1] // depth)
    def _(i):
        span = pl.ds(pl.multiple_of(i * depth, depth), depth)
        left = jnp.concatenate([p[:rows, span] for p in parts], axis=0)
        right = jnp.concatenate([w[:, span] for w in weights], axis=0)
        total[...] += lax.dot_general(left, right, NT, preferred_element_type=jnp.float32)

    width = total.shape[1]
    for b in range(blocks):
        for g in range(rows // SLAB):
            top = b * rows + g * SLAB
            outs[b][:, g * width : (g + 1) * width] = total[top : top + SLAB].astype(jnp.bfloat16)


def project(parts, rows, weights):
    width = QUAD * weights[0].shape[0]
    vmem = pl.BlockSpec(memory_space=pltpu.VMEM)
    total = jax.ShapeDtypeStruct((rows * len(parts), width), jnp.float32)
    return pl.pallas_call(
        functools.partial(project_kernel, len(parts), rows),
        out_shape=[jax.ShapeDtypeStruct((SLAB, rows // SLAB * width), jnp.bfloat16)] * len(parts),
        in_specs=[vmem] * (len(parts) + QUAD),
        out_specs=[vmem] * len(parts),
        scratch_shapes=[pltpu.VMEM(total.shape, total.dtype)],
        cost_estimate=SMALL,
        compiler_params=pltpu.CompilerParams(vmem_limit_bytes=room(*parts, *weights, total, total)),
        name="project",
    )(*parts, *weights)


def assemble_kernel(planes, groups, here_ref, mine_ref, over_y_ref, rest_ref, out_ref):
    span = mine_ref.shape[0]
    rows, columns = span // planes, out_ref.shape[1] // groups
    sources = (mine_ref, rest_ref, over_y_ref, rest_ref)
    for rel in range(QUAD):
        base = span if rel == 3 else 0
        for d in range(planes):
            home = (here_ref[0] ^ d) * QUAD + (here_ref[1] ^ rel)
            row = pl.multiple_of(home * rows, rows)
            for k in range(groups):
                column = pl.multiple_of(lax.rem(here_ref[2] + (groups - k), groups) * columns, columns)
                out_ref[pl.ds(row, rows), pl.ds(column, columns)] = sources[rel][
                    base + d * rows : base + (d + 1) * rows, k * columns : (k + 1) * columns
                ]


def assemble(here, mine, over_y, rest, planes, groups):
    span, width = mine.shape
    vmem = pl.BlockSpec(memory_space=pltpu.VMEM)
    return pl.pallas_call(
        functools.partial(assemble_kernel, planes, groups),
        out_shape=jax.ShapeDtypeStruct((span * QUAD, width), mine.dtype),
        in_specs=[pl.BlockSpec(memory_space=pltpu.SMEM), vmem, vmem, vmem],
        out_specs=vmem,
        cost_estimate=SMALL,
        compiler_params=pltpu.CompilerParams(vmem_limit_bytes=room(mine, mine, mine, mine, mine, over_y, rest)),
        name="assemble",
    )(here, mine, over_y, rest)


def after(array, *others):
    return lax.optimization_barrier((array, *others))[0]


def shards(tokens, out_grad, routes, route_weight, example_ids, in_proj, out_proj, queries):
    token_count, model_width = tokens.shape
    owned = in_proj.shape[0]
    n, groups = lax.axis_size("expert"), lax.axis_size("groups")
    planes = n // QUAD
    me, group = lax.axis_index("expert"), lax.axis_index("groups")
    plane, spot = me // QUAD, me % QUAD

    def move(array, hops):
        pairs = [(a * QUAD + q, b * QUAD + q) for a, b in hops for q in range(QUAD)]
        return lax.ppermute(array, "expert", pairs)

    def swap(array, bit):
        return lax.ppermute(array, "expert", [(i, i ^ bit) for i in range(n)])

    weights = jnp.swapaxes(in_proj, 1, 2).reshape(owned * RANK, model_width)

    ways_home = []
    for s in range(1, planes):
        up_home = [(p, p - s) for p in range(s, planes)]
        down_home = [(p, p + s) for p in range(planes - s)]
        ways_home.extend([up_home + down_home] if 2 * s >= planes else [up_home, down_home])

    homes = []
    for home in ways_home:
        back = -jnp.ones((), jnp.int32)
        for a, b in home:
            back = jnp.where(plane == b, a, back)
        homes.append(back)
    grad_side = jnp.dot(out_grad, out_proj, preferred_element_type=jnp.float32)
    rel = jnp.arange(QUAD, dtype=jnp.int32)
    inner = ((spot ^ rel)[:, None] * owned + jnp.arange(owned, dtype=jnp.int32)[None, :]).reshape(-1)
    place = jnp.stack([plane] + homes)
    expert_ids = jnp.where(place[:, None] >= 0, place[:, None] * (QUAD * owned) + inner[None, :], -1).reshape(-1)
    gate = jnp.sum(
        jnp.where(routes.T[None, :, :] == expert_ids[:, None, None], route_weight.T[None, :, :], 0.0), axis=1
    )
    local_ids = example_ids.reshape(token_count)
    member = local_ids[:, None] == jnp.arange(EX_DEV, dtype=jnp.int32)[None, :]
    counts = jnp.sum(member.astype(jnp.float32), axis=0)
    counts = jnp.broadcast_to(counts[:, None], (EX_DEV, RANK))
    repeated = jnp.concatenate([grad_side] * EX_DEV, axis=1)
    widely = jnp.repeat(member, RANK, axis=1)
    experts = QUAD * owned

    def widen(part):
        spread = (part[:, :, None] * repeated[None]).astype(jnp.bfloat16)
        return jnp.where(widely[None], spread, jnp.zeros((), jnp.bfloat16))

    wide, wide_late = widen(gate[:-experts]), widen(gate[-experts:])

    over_y = swap(weights, 2)

    width = queries.shape[1] // groups
    lined = lax.dynamic_slice_in_dim(queries, group * width, width, axis=1)
    lined = jnp.concatenate([lined, swap(lined, QUAD)], axis=0)

    middle = (planes + 1) // 2
    up, down = tokens, tokens
    first = []
    for s in range(1, middle):
        up, down = move(up, [(p, p + 1) for p in range(s - 1, planes - 1)]), move(
            down, [(p, p - 1) for p in range(1, planes - s + 1)]
        )
        first.extend([up, down])
    over_core = swap(weights, 1)
    lined = after(lined, wide, wide_late, *first)
    bit = 2 * QUAD
    while bit < n:
        lined = jnp.concatenate([lined, swap(lined, bit)], axis=0)
        bit *= 2

    for s in range(middle, planes):
        up_hops = [(p, p + 1) for p in range(s - 1, planes - 1)]
        down_hops = [(p, p - 1) for p in range(1, planes - s + 1)]
        if s == middle:
            up, down = move(up, up_hops), move(down, down_hops)
            up = down = up + after(down, lined)
            across = swap(after(over_y, up), 1)
            quad_weights = [weights, over_core, over_y, across]
            lined = after(lined, up)
            ranged = [lined] + [
                lax.ppermute(lined, "groups", [(g, (g + k) % groups) for g in range(groups)]) for k in range(1, groups)
            ]
            own, *sides = project([tokens] + first + [up], token_count, quad_weights)
            returned = [move(side, home) for side, home in zip(sides, ways_home)]
            mine = jnp.concatenate(after(tuple(ranged), own), axis=1)
            mine_over_y = swap(mine, 2)
        else:
            up = down = move(up, up_hops + down_hops)
            wait = returned if s == planes - 1 else []
            (side,) = project([after(up, *wait)], token_count, quad_weights)
            returned.append(move(side, ways_home[len(returned)]))
    late = returned.pop()
    early = combine([own] + returned, wide)

    rest = swap(after(jnp.concatenate([mine, mine_over_y], axis=0), late), 1)
    here = jnp.stack([plane, spot, group]).astype(jnp.int32)
    all_queries = assemble(here, mine, mine_over_y, rest, planes, groups)
    sketches = combine([late], wide_late, early, counts)
    sketches = sketches.reshape(EX_DEV, RANK * RANK)
    scores = lax.dot_general(sketches.astype(jnp.bfloat16), all_queries, NT, preferred_element_type=jnp.float32)
    return (sketches, scores)


def solution(mesh):
    placed = (
        P(("groups", "expert"), None),
        P(("groups", "expert"), None),
        P(("groups", "expert"), None),
        P(("groups", "expert"), None),
        P(("groups", "expert"), None),
        P("expert", None, None),
        P(),
        P("expert", None),
    )
    return jax.shard_map(
        shards,
        mesh=mesh,
        in_specs=placed,
        out_specs=(P(("groups", "expert"), None), P(("groups", "expert"), None)),
        check_vma=False,
    )
```

```python
import functools
import math

import jax
import jax.numpy as jnp
from jax import lax
from jax.experimental import pallas as pl
from jax.experimental.pallas import tpu as pltpu
from jax.sharding import PartitionSpec as P

RANK = 64
EX_DEV = 4
QUAD = 4
SLAB = 16

SMALL = pl.CostEstimate(flops=1024, bytes_accessed=1024, transcendentals=0)

NT = (((1,), (1,)), ((), ()))
TN = (((0,), (0,)), ((), ()))


def room(*arrays):
    return sum(math.prod(a.shape) * jnp.dtype(a.dtype).itemsize for a in arrays) + (6 << 20)


def combine_kernel(blocks, experts, first, last, *refs):
    sides, wide = refs[:blocks], refs[blocks]
    total = jnp.zeros((RANK, EX_DEV * RANK), jnp.float32) if first else refs[blocks + 1][...]
    out = refs[-1]
    span = experts * RANK
    for b in range(blocks):
        slabs = [sides[b][:, g * span : (g + 1) * span] for g in range(wide.shape[1] // SLAB)]
        side = jnp.concatenate(slabs, axis=0)
        for e in range(experts):
            total += lax.dot_general(
                side[:, e * RANK : (e + 1) * RANK],
                wide[b * experts + e],
                TN,
                preferred_element_type=jnp.float32,
            )
    if last:
        counts = refs[-2]
        for x in range(EX_DEV):
            out[x] = total[:, x * RANK : (x + 1) * RANK] / counts[x : x + 1, :]
    else:
        out[...] = total


def combine(sides, wide, total=None, counts=None):
    experts = wide.shape[0] // len(sides)
    extra = [a for a in (total, counts) if a is not None]
    shape = (RANK, EX_DEV * RANK) if counts is None else (EX_DEV, RANK, RANK)
    return pl.pallas_call(
        functools.partial(combine_kernel, len(sides), experts, total is None, counts is not None),
        out_shape=jax.ShapeDtypeStruct(shape, jnp.float32),
        in_specs=[pl.BlockSpec(memory_space=pltpu.VMEM)] * (len(sides) + 1 + len(extra)),
        out_specs=pl.BlockSpec(memory_space=pltpu.VMEM),
        cost_estimate=SMALL,
        compiler_params=pltpu.CompilerParams(vmem_limit_bytes=room(*sides, wide)),
        name="combine",
    )(*sides, wide, *extra)


def project_kernel(blocks, rows, *refs):
    parts, weights = refs[:blocks], refs[blocks : blocks + QUAD]
    outs, total = refs[blocks + QUAD : -1], refs[-1]
    depth = 1024
    total[...] = jnp.zeros_like(total)

    @pl.loop(0, parts[0].shape[1] // depth)
    def _(i):
        span = pl.ds(pl.multiple_of(i * depth, depth), depth)
        left = jnp.concatenate([p[:rows, span] for p in parts], axis=0)
        right = jnp.concatenate([w[:, span] for w in weights], axis=0)
        total[...] += lax.dot_general(left, right, NT, preferred_element_type=jnp.float32)

    width = total.shape[1]
    for b in range(blocks):
        for g in range(rows // SLAB):
            top = b * rows + g * SLAB
            outs[b][:, g * width : (g + 1) * width] = total[top : top + SLAB].astype(jnp.bfloat16)


def project(parts, rows, weights):
    width = QUAD * weights[0].shape[0]
    vmem = pl.BlockSpec(memory_space=pltpu.VMEM)
    total = jax.ShapeDtypeStruct((rows * len(parts), width), jnp.float32)
    return pl.pallas_call(
        functools.partial(project_kernel, len(parts), rows),
        out_shape=[jax.ShapeDtypeStruct((SLAB, rows // SLAB * width), jnp.bfloat16)] * len(parts),
        in_specs=[vmem] * (len(parts) + QUAD),
        out_specs=[vmem] * len(parts),
        scratch_shapes=[pltpu.VMEM(total.shape, total.dtype)],
        cost_estimate=SMALL,
        compiler_params=pltpu.CompilerParams(vmem_limit_bytes=room(*parts, *weights, total, total)),
        name="project",
    )(*parts, *weights)


def assemble_kernel(order, groups, here_ref, mine_ref, over_y_ref, rest_ref, out_ref):
    span = mine_ref.shape[0]
    rows, columns = span // len(order), out_ref.shape[1] // groups
    sources = (mine_ref, rest_ref, over_y_ref, rest_ref)
    for rel in range(QUAD):
        base = span if rel == 3 else 0
        for d, other in enumerate(order):
            home = (here_ref[0] ^ other) * QUAD + (here_ref[1] ^ rel)
            row = pl.multiple_of(home * rows, rows)
            for k in range(groups):
                column = pl.multiple_of(lax.rem(here_ref[2] + (groups - k), groups) * columns, columns)
                out_ref[pl.ds(row, rows), pl.ds(column, columns)] = sources[rel][
                    base + d * rows : base + (d + 1) * rows, k * columns : (k + 1) * columns
                ]


def assemble(here, mine, over_y, rest, order, groups):
    span, width = mine.shape
    vmem = pl.BlockSpec(memory_space=pltpu.VMEM)
    return pl.pallas_call(
        functools.partial(assemble_kernel, order, groups),
        out_shape=jax.ShapeDtypeStruct((span * QUAD, width), mine.dtype),
        in_specs=[pl.BlockSpec(memory_space=pltpu.SMEM), vmem, vmem, vmem],
        out_specs=vmem,
        cost_estimate=SMALL,
        compiler_params=pltpu.CompilerParams(vmem_limit_bytes=room(mine, mine, mine, mine, mine, over_y, rest)),
        name="assemble",
    )(here, mine, over_y, rest)


def after(array, *others):
    return lax.optimization_barrier((array, *others))[0]


def shards(tokens, out_grad, routes, route_weight, example_ids, in_proj, out_proj, queries):
    token_count, model_width = tokens.shape
    owned = in_proj.shape[0]
    n, groups = lax.axis_size("expert"), lax.axis_size("groups")
    planes = n // QUAD
    me, group = lax.axis_index("expert"), lax.axis_index("groups")
    plane, spot = me // QUAD, me % QUAD

    def move(array, hops):
        pairs = [(a * QUAD + q, b * QUAD + q) for a, b in hops for q in range(QUAD)]
        return lax.ppermute(array, "expert", pairs)

    def swap(array, bit):
        return lax.ppermute(array, "expert", [(i, i ^ bit) for i in range(n)])

    weights = jnp.swapaxes(in_proj, 1, 2).reshape(owned * RANK, model_width)

    ways_home = []
    for s in range(1, planes):
        up_home = [(p, p - s) for p in range(s, planes)]
        down_home = [(p, p + s) for p in range(planes - s)]
        ways_home.extend([up_home + down_home] if 2 * s >= planes else [up_home, down_home])

    homes = []
    for home in ways_home:
        back = -jnp.ones((), jnp.int32)
        for a, b in home:
            back = jnp.where(plane == b, a, back)
        homes.append(back)
    grad_side = jnp.dot(out_grad, out_proj, preferred_element_type=jnp.float32)
    rel = jnp.arange(QUAD, dtype=jnp.int32)
    inner = ((spot ^ rel)[:, None] * owned + jnp.arange(owned, dtype=jnp.int32)[None, :]).reshape(-1)
    place = jnp.stack([plane] + homes)
    expert_ids = jnp.where(place[:, None] >= 0, place[:, None] * (QUAD * owned) + inner[None, :], -1).reshape(-1)
    gate = jnp.sum(
        jnp.where(routes.T[None, :, :] == expert_ids[:, None, None], route_weight.T[None, :, :], 0.0), axis=1
    )
    local_ids = example_ids.reshape(token_count)
    member = local_ids[:, None] == jnp.arange(EX_DEV, dtype=jnp.int32)[None, :]
    counts = jnp.sum(member.astype(jnp.float32), axis=0)
    counts = jnp.broadcast_to(counts[:, None], (EX_DEV, RANK))
    repeated = jnp.concatenate([grad_side] * EX_DEV, axis=1)
    widely = jnp.repeat(member, RANK, axis=1)
    experts = QUAD * owned

    def widen(part):
        spread = (part[:, :, None] * repeated[None]).astype(jnp.bfloat16)
        return jnp.where(widely[None], spread, jnp.zeros((), jnp.bfloat16))

    wide, wide_late = widen(gate[:-experts]), widen(gate[-experts:])

    over_y = swap(weights, 2)

    width = queries.shape[1] // groups
    lined = lax.dynamic_slice_in_dim(queries, group * width, width, axis=1)
    bit, order = planes // 2, [0]
    lined = jnp.concatenate([lined, swap(lined, bit * QUAD)], axis=0)
    order = order + [o ^ bit for o in order]

    middle = (planes + 1) // 2
    up, down = tokens, tokens
    first = []
    for s in range(1, middle):
        up, down = move(up, [(p, p + 1) for p in range(s - 1, planes - 1)]), move(
            down, [(p, p - 1) for p in range(1, planes - s + 1)]
        )
        first.extend([up, down])
    over_core = swap(weights, 1)
    lined = after(lined, wide, wide_late, *first)
    bit //= 2
    while bit:
        lined = jnp.concatenate([lined, swap(lined, bit * QUAD)], axis=0)
        order = order + [o ^ bit for o in order]
        bit //= 2

    for s in range(middle, planes):
        up_hops = [(p, p + 1) for p in range(s - 1, planes - 1)]
        down_hops = [(p, p - 1) for p in range(1, planes - s + 1)]
        if s == middle:
            up, down = move(up, up_hops), move(down, down_hops)
            up = down = up + after(down, lined)
            across = swap(after(over_y, up), 1)
            quad_weights = [weights, over_core, over_y, across]
            lined = after(lined, up)
            ranged = [lined] + [
                lax.ppermute(lined, "groups", [(g, (g + k) % groups) for g in range(groups)]) for k in range(1, groups)
            ]
            own, *sides = project([tokens] + first + [up], token_count, quad_weights)
            returned = [move(side, home) for side, home in zip(sides, ways_home)]
            mine = jnp.concatenate(after(tuple(ranged), own), axis=1)
            mine_over_y = swap(mine, 2)
        else:
            up = down = move(up, up_hops + down_hops)
            wait = returned if s == planes - 1 else []
            (side,) = project([after(up, *wait)], token_count, quad_weights)
            returned.append(move(side, ways_home[len(returned)]))
    late = returned.pop()
    early = combine([own] + returned, wide)

    rest = swap(after(jnp.concatenate([mine, mine_over_y], axis=0), late), 1)
    here = jnp.stack([plane, spot, group]).astype(jnp.int32)
    all_queries = assemble(here, mine, mine_over_y, rest, order, groups)
    sketches = combine([late], wide_late, early, counts)
    sketches = sketches.reshape(EX_DEV, RANK * RANK)
    scores = lax.dot_general(sketches.astype(jnp.bfloat16), all_queries, NT, preferred_element_type=jnp.float32)
    return (sketches, scores)


def solution(mesh):
    placed = (
        P(("groups", "expert"), None),
        P(("groups", "expert"), None),
        P(("groups", "expert"), None),
        P(("groups", "expert"), None),
        P(("groups", "expert"), None),
        P("expert", None, None),
        P(),
        P("expert", None),
    )
    return jax.shard_map(
        shards,
        mesh=mesh,
        in_specs=placed,
        out_specs=(P(("groups", "expert"), None), P(("groups", "expert"), None)),
        check_vma=False,
    )
```

```python
import functools
import math

import jax
import jax.numpy as jnp
from jax import lax
from jax.experimental import pallas as pl
from jax.experimental.pallas import tpu as pltpu
from jax.sharding import PartitionSpec as P

RANK = 64
EX_DEV = 4
QUAD = 4
SLAB = 16

SMALL = pl.CostEstimate(flops=1024, bytes_accessed=1024, transcendentals=0)

NT = (((1,), (1,)), ((), ()))
TN = (((0,), (0,)), ((), ()))


def room(*arrays):
    return sum(math.prod(a.shape) * jnp.dtype(a.dtype).itemsize for a in arrays) + (6 << 20)


def combine_kernel(blocks, experts, first, last, *refs):
    sides, wide = refs[:blocks], refs[blocks]
    total = jnp.zeros((RANK, EX_DEV * RANK), jnp.float32) if first else refs[blocks + 1][...]
    out = refs[-1]
    span = experts * RANK
    for b in range(blocks):
        slabs = [sides[b][:, g * span : (g + 1) * span] for g in range(wide.shape[1] // SLAB)]
        side = jnp.concatenate(slabs, axis=0)
        for e in range(experts):
            total += lax.dot_general(
                side[:, e * RANK : (e + 1) * RANK],
                wide[b * experts + e],
                TN,
                preferred_element_type=jnp.float32,
            )
    if last:
        counts = refs[-2]
        for x in range(EX_DEV):
            out[x] = total[:, x * RANK : (x + 1) * RANK] / counts[x : x + 1, :]
    else:
        out[...] = total


def combine(sides, wide, total=None, counts=None):
    experts = wide.shape[0] // len(sides)
    extra = [a for a in (total, counts) if a is not None]
    shape = (RANK, EX_DEV * RANK) if counts is None else (EX_DEV, RANK, RANK)
    return pl.pallas_call(
        functools.partial(combine_kernel, len(sides), experts, total is None, counts is not None),
        out_shape=jax.ShapeDtypeStruct(shape, jnp.float32),
        in_specs=[pl.BlockSpec(memory_space=pltpu.VMEM)] * (len(sides) + 1 + len(extra)),
        out_specs=pl.BlockSpec(memory_space=pltpu.VMEM),
        cost_estimate=SMALL,
        compiler_params=pltpu.CompilerParams(vmem_limit_bytes=room(*sides, wide)),
        name="combine",
    )(*sides, wide, *extra)


def project_kernel(blocks, rows, *refs):
    parts, weights = refs[:blocks], refs[blocks : blocks + QUAD]
    outs, total = refs[blocks + QUAD : -1], refs[-1]
    left = jnp.concatenate([p[...] for p in parts], axis=0)
    right = jnp.concatenate([w[...] for w in weights], axis=0)
    product = lax.dot_general(left, right, NT, preferred_element_type=jnp.float32)

    @pl.when(pl.program_id(0) == 0)
    def _():
        total[...] = product

    @pl.when(pl.program_id(0) > 0)
    def _():
        total[...] += product

    @pl.when(pl.program_id(0) == pl.num_programs(0) - 1)
    def _():
        width = total.shape[1]
        for b in range(blocks):
            for g in range(rows // SLAB):
                top = b * rows + g * SLAB
                outs[b][:, g * width : (g + 1) * width] = total[top : top + SLAB].astype(jnp.bfloat16)


def project(parts, rows, weights):
    width, depth = QUAD * weights[0].shape[0], 1024
    total = jax.ShapeDtypeStruct((rows * len(parts), width), jnp.float32)
    side = (SLAB, rows // SLAB * width)
    return pl.pallas_call(
        functools.partial(project_kernel, len(parts), rows),
        grid=(parts[0].shape[1] // depth,),
        out_shape=[jax.ShapeDtypeStruct(side, jnp.bfloat16)] * len(parts),
        in_specs=[pl.BlockSpec((a.shape[0], depth), lambda i: (0, i)) for a in (*parts, *weights)],
        out_specs=[pl.BlockSpec(side, lambda i: (0, 0))] * len(parts),
        scratch_shapes=[pltpu.VMEM(total.shape, total.dtype)],
        cost_estimate=SMALL,
        compiler_params=pltpu.CompilerParams(vmem_limit_bytes=room(*parts, *weights, total, total)),
        name="project",
    )(*parts, *weights)


def assemble_kernel(order, groups, here_ref, mine_ref, over_y_ref, rest_ref, out_ref):
    span = mine_ref.shape[0]
    rows, columns = span // len(order), out_ref.shape[1] // groups
    sources = (mine_ref, rest_ref, over_y_ref, rest_ref)
    for rel in range(QUAD):
        base = span if rel == 3 else 0
        for d, other in enumerate(order):
            home = (here_ref[0] ^ other) * QUAD + (here_ref[1] ^ rel)
            row = pl.multiple_of(home * rows, rows)
            for k in range(groups):
                column = pl.multiple_of(lax.rem(here_ref[2] + (groups - k), groups) * columns, columns)
                out_ref[pl.ds(row, rows), pl.ds(column, columns)] = sources[rel][
                    base + d * rows : base + (d + 1) * rows, k * columns : (k + 1) * columns
                ]


def assemble(here, mine, over_y, rest, order, groups):
    span, width = mine.shape
    vmem = pl.BlockSpec(memory_space=pltpu.VMEM)
    return pl.pallas_call(
        functools.partial(assemble_kernel, order, groups),
        out_shape=jax.ShapeDtypeStruct((span * QUAD, width), mine.dtype),
        in_specs=[pl.BlockSpec(memory_space=pltpu.SMEM), vmem, vmem, vmem],
        out_specs=vmem,
        cost_estimate=SMALL,
        compiler_params=pltpu.CompilerParams(vmem_limit_bytes=room(mine, mine, mine, mine, mine, over_y, rest)),
        name="assemble",
    )(here, mine, over_y, rest)


def after(array, *others):
    return lax.optimization_barrier((array, *others))[0]


def shards(tokens, out_grad, routes, route_weight, example_ids, in_proj, out_proj, queries):
    token_count, model_width = tokens.shape
    owned = in_proj.shape[0]
    n, groups = lax.axis_size("expert"), lax.axis_size("groups")
    planes = n // QUAD
    me, group = lax.axis_index("expert"), lax.axis_index("groups")
    plane, spot = me // QUAD, me % QUAD

    def move(array, hops):
        pairs = [(a * QUAD + q, b * QUAD + q) for a, b in hops for q in range(QUAD)]
        return lax.ppermute(array, "expert", pairs)

    def swap(array, bit):
        return lax.ppermute(array, "expert", [(i, i ^ bit) for i in range(n)])

    weights = jnp.swapaxes(in_proj, 1, 2).reshape(owned * RANK, model_width)

    ways_home = []
    for s in range(1, planes):
        up_home = [(p, p - s) for p in range(s, planes)]
        down_home = [(p, p + s) for p in range(planes - s)]
        ways_home.extend([up_home + down_home] if 2 * s >= planes else [up_home, down_home])

    homes = []
    for home in ways_home:
        back = -jnp.ones((), jnp.int32)
        for a, b in home:
            back = jnp.where(plane == b, a, back)
        homes.append(back)
    grad_side = jnp.dot(out_grad, out_proj, preferred_element_type=jnp.float32)
    rel = jnp.arange(QUAD, dtype=jnp.int32)
    inner = ((spot ^ rel)[:, None] * owned + jnp.arange(owned, dtype=jnp.int32)[None, :]).reshape(-1)
    place = jnp.stack([plane] + homes)
    expert_ids = jnp.where(place[:, None] >= 0, place[:, None] * (QUAD * owned) + inner[None, :], -1).reshape(-1)
    gate = jnp.sum(
        jnp.where(routes.T[None, :, :] == expert_ids[:, None, None], route_weight.T[None, :, :], 0.0), axis=1
    )
    local_ids = example_ids.reshape(token_count)
    member = local_ids[:, None] == jnp.arange(EX_DEV, dtype=jnp.int32)[None, :]
    counts = jnp.sum(member.astype(jnp.float32), axis=0)
    counts = jnp.broadcast_to(counts[:, None], (EX_DEV, RANK))
    repeated = jnp.concatenate([grad_side] * EX_DEV, axis=1)
    widely = jnp.repeat(member, RANK, axis=1)
    experts = QUAD * owned

    def widen(part):
        spread = (part[:, :, None] * repeated[None]).astype(jnp.bfloat16)
        return jnp.where(widely[None], spread, jnp.zeros((), jnp.bfloat16))

    wide, wide_late = widen(gate[:-experts]), widen(gate[-experts:])

    over_y = swap(weights, 2)

    width = queries.shape[1] // groups
    lined = lax.dynamic_slice_in_dim(queries, group * width, width, axis=1)
    bit, order = planes // 2, [0]
    lined = jnp.concatenate([lined, swap(lined, bit * QUAD)], axis=0)
    order = order + [o ^ bit for o in order]

    middle = (planes + 1) // 2
    up, down = tokens, tokens
    first = []
    for s in range(1, middle):
        up, down = move(up, [(p, p + 1) for p in range(s - 1, planes - 1)]), move(
            down, [(p, p - 1) for p in range(1, planes - s + 1)]
        )
        first.extend([up, down])
    over_core = swap(weights, 1)
    lined = after(lined, wide, wide_late, *first)
    bit //= 2
    while bit:
        lined = jnp.concatenate([lined, swap(lined, bit * QUAD)], axis=0)
        order = order + [o ^ bit for o in order]
        bit //= 2

    for s in range(middle, planes):
        up_hops = [(p, p + 1) for p in range(s - 1, planes - 1)]
        down_hops = [(p, p - 1) for p in range(1, planes - s + 1)]
        if s == middle:
            up, down = move(up, up_hops), move(down, down_hops)
            up = down = up + after(down, lined)
            across = swap(after(over_y, up), 1)
            quad_weights = [weights, over_core, over_y, across]
            lined = after(lined, up)
            ranged = [lined] + [
                lax.ppermute(lined, "groups", [(g, (g + k) % groups) for g in range(groups)]) for k in range(1, groups)
            ]
            own, *sides = project([tokens] + first + [up], token_count, quad_weights)
            returned = [move(side, home) for side, home in zip(sides, ways_home)]
            mine = jnp.concatenate(after(tuple(ranged), own), axis=1)
            mine_over_y = swap(mine, 2)
        else:
            up = down = move(up, up_hops + down_hops)
            wait = returned if s == planes - 1 else []
            (side,) = project([after(up, *wait)], token_count, quad_weights)
            returned.append(move(side, ways_home[len(returned)]))
    late = returned.pop()
    early = combine([own] + returned, wide)

    rest = swap(after(jnp.concatenate([mine, mine_over_y], axis=0), side), 1)
    here = jnp.stack([plane, spot, group]).astype(jnp.int32)
    all_queries = assemble(here, mine, mine_over_y, rest, order, groups)
    sketches = combine([late], wide_late, early, counts)
    sketches = sketches.reshape(EX_DEV, RANK * RANK)
    scores = lax.dot_general(sketches.astype(jnp.bfloat16), all_queries, NT, preferred_element_type=jnp.float32)
    return (sketches, scores)


def solution(mesh):
    placed = (
        P(("groups", "expert"), None),
        P(("groups", "expert"), None),
        P(("groups", "expert"), None),
        P(("groups", "expert"), None),
        P(("groups", "expert"), None),
        P("expert", None, None),
        P(),
        P("expert", None),
    )
    return jax.shard_map(
        shards,
        mesh=mesh,
        in_specs=placed,
        out_specs=(P(("groups", "expert"), None), P(("groups", "expert"), None)),
        check_vma=False,
    )
```

```python
import functools
import math

import jax
import jax.numpy as jnp
from jax import lax
from jax.experimental import pallas as pl
from jax.experimental.pallas import tpu as pltpu
from jax.sharding import PartitionSpec as P

RANK = 64
EX_DEV = 4
QUAD = 4
SLAB = 16

SMALL = pl.CostEstimate(flops=1024, bytes_accessed=1024, transcendentals=0)

NT = (((1,), (1,)), ((), ()))
TN = (((0,), (0,)), ((), ()))


def room(*arrays):
    return sum(math.prod(a.shape) * jnp.dtype(a.dtype).itemsize for a in arrays) + (6 << 20)


def combine_kernel(blocks, experts, first, last, *refs):
    sides, wide = refs[:blocks], refs[blocks]
    total = jnp.zeros((RANK, EX_DEV * RANK), jnp.float32) if first else refs[blocks + 1][...]
    out = refs[-1]
    span = experts * RANK
    for b in range(blocks):
        slabs = [sides[b][:, g * span : (g + 1) * span] for g in range(wide.shape[1] // SLAB)]
        side = jnp.concatenate(slabs, axis=0)
        for e in range(experts):
            total += lax.dot_general(
                side[:, e * RANK : (e + 1) * RANK],
                wide[b * experts + e],
                TN,
                preferred_element_type=jnp.float32,
            )
    if last:
        counts = refs[-2]
        for x in range(EX_DEV):
            out[x] = total[:, x * RANK : (x + 1) * RANK] / counts[x : x + 1, :]
    else:
        out[...] = total


def combine(sides, wide, total=None, counts=None):
    experts = wide.shape[0] // len(sides)
    extra = [a for a in (total, counts) if a is not None]
    shape = (RANK, EX_DEV * RANK) if counts is None else (EX_DEV, RANK, RANK)
    return pl.pallas_call(
        functools.partial(combine_kernel, len(sides), experts, total is None, counts is not None),
        out_shape=jax.ShapeDtypeStruct(shape, jnp.float32),
        in_specs=[pl.BlockSpec(memory_space=pltpu.VMEM)] * (len(sides) + 1 + len(extra)),
        out_specs=pl.BlockSpec(memory_space=pltpu.VMEM),
        cost_estimate=SMALL,
        compiler_params=pltpu.CompilerParams(vmem_limit_bytes=room(*sides, wide)),
        name="combine",
    )(*sides, wide, *extra)


def project_kernel(blocks, rows, *refs):
    parts, weights = refs[:blocks], refs[blocks : blocks + QUAD]
    outs, total = refs[blocks + QUAD : -1], refs[-1]
    depth = 1024
    total[...] = jnp.zeros_like(total)

    @pl.loop(0, parts[0].shape[1] // depth)
    def _(i):
        span = pl.ds(pl.multiple_of(i * depth, depth), depth)
        left = jnp.concatenate([p[:rows, span] for p in parts], axis=0)
        right = jnp.concatenate([w[:, span] for w in weights], axis=0)
        total[...] += lax.dot_general(left, right, NT, preferred_element_type=jnp.float32)

    width = total.shape[1]
    for b in range(blocks):
        for g in range(rows // SLAB):
            top = b * rows + g * SLAB
            outs[b][:, g * width : (g + 1) * width] = total[top : top + SLAB].astype(jnp.bfloat16)


def project(parts, rows, weights):
    width = QUAD * weights[0].shape[0]
    vmem = pl.BlockSpec(memory_space=pltpu.VMEM)
    total = jax.ShapeDtypeStruct((rows * len(parts), width), jnp.float32)
    return pl.pallas_call(
        functools.partial(project_kernel, len(parts), rows),
        out_shape=[jax.ShapeDtypeStruct((SLAB, rows // SLAB * width), jnp.bfloat16)] * len(parts),
        in_specs=[vmem] * (len(parts) + QUAD),
        out_specs=[vmem] * len(parts),
        scratch_shapes=[pltpu.VMEM(total.shape, total.dtype)],
        cost_estimate=SMALL,
        compiler_params=pltpu.CompilerParams(vmem_limit_bytes=room(*parts, *weights, total, total)),
        name="project",
    )(*parts, *weights)


def assemble_kernel(order, groups, here_ref, mine_ref, over_y_ref, rest_ref, out_ref):
    span = mine_ref.shape[0]
    rows, columns = span // len(order), out_ref.shape[1] // groups
    sources = (mine_ref, rest_ref, over_y_ref, rest_ref)
    for rel in range(QUAD):
        base = span if rel == 3 else 0
        for d, other in enumerate(order):
            home = (here_ref[0] ^ other) * QUAD + (here_ref[1] ^ rel)
            row = pl.multiple_of(home * rows, rows)
            for k in range(groups):
                column = pl.multiple_of(lax.rem(here_ref[2] + (groups - k), groups) * columns, columns)
                out_ref[pl.ds(row, rows), pl.ds(column, columns)] = sources[rel][
                    base + d * rows : base + (d + 1) * rows, k * columns : (k + 1) * columns
                ]


def assemble(here, mine, over_y, rest, order, groups):
    span, width = mine.shape
    vmem = pl.BlockSpec(memory_space=pltpu.VMEM)
    return pl.pallas_call(
        functools.partial(assemble_kernel, order, groups),
        out_shape=jax.ShapeDtypeStruct((span * QUAD, width), mine.dtype),
        in_specs=[pl.BlockSpec(memory_space=pltpu.SMEM), vmem, vmem, vmem],
        out_specs=vmem,
        cost_estimate=SMALL,
        compiler_params=pltpu.CompilerParams(vmem_limit_bytes=room(mine, mine, mine, mine, mine, over_y, rest)),
        name="assemble",
    )(here, mine, over_y, rest)


def after(array, *others):
    return lax.optimization_barrier((array, *others))[0]


def shards(tokens, out_grad, routes, route_weight, example_ids, in_proj, out_proj, queries):
    token_count, model_width = tokens.shape
    owned = in_proj.shape[0]
    n, groups = lax.axis_size("expert"), lax.axis_size("groups")
    planes = n // QUAD
    me, group = lax.axis_index("expert"), lax.axis_index("groups")
    plane, spot = me // QUAD, me % QUAD

    def move(array, hops):
        pairs = [(a * QUAD + q, b * QUAD + q) for a, b in hops for q in range(QUAD)]
        return lax.ppermute(array, "expert", pairs)

    def swap(array, bit):
        return lax.ppermute(array, "expert", [(i, i ^ bit) for i in range(n)])

    weights = jnp.swapaxes(in_proj, 1, 2).reshape(owned * RANK, model_width)

    ways_home = []
    for s in range(1, planes):
        up_home = [(p, p - s) for p in range(s, planes)]
        down_home = [(p, p + s) for p in range(planes - s)]
        ways_home.extend([up_home + down_home] if 2 * s >= planes else [up_home, down_home])

    homes = []
    for home in ways_home:
        back = -jnp.ones((), jnp.int32)
        for a, b in home:
            back = jnp.where(plane == b, a, back)
        homes.append(back)
    grad_side = jnp.dot(out_grad, out_proj, preferred_element_type=jnp.float32)
    rel = jnp.arange(QUAD, dtype=jnp.int32)
    inner = ((spot ^ rel)[:, None] * owned + jnp.arange(owned, dtype=jnp.int32)[None, :]).reshape(-1)
    place = jnp.stack([plane] + homes)
    expert_ids = jnp.where(place[:, None] >= 0, place[:, None] * (QUAD * owned) + inner[None, :], -1).reshape(-1)
    gate = jnp.sum(
        jnp.where(routes.T[None, :, :] == expert_ids[:, None, None], route_weight.T[None, :, :], 0.0), axis=1
    )
    local_ids = example_ids.reshape(token_count)
    member = local_ids[:, None] == jnp.arange(EX_DEV, dtype=jnp.int32)[None, :]
    counts = jnp.sum(member.astype(jnp.float32), axis=0)
    counts = jnp.broadcast_to(counts[:, None], (EX_DEV, RANK))
    repeated = jnp.concatenate([grad_side] * EX_DEV, axis=1)
    widely = jnp.repeat(member, RANK, axis=1)
    experts = QUAD * owned

    def widen(part):
        spread = (part[:, :, None] * repeated[None]).astype(jnp.bfloat16)
        return jnp.where(widely[None], spread, jnp.zeros((), jnp.bfloat16))

    wide, wide_late = widen(gate[:-experts]), widen(gate[-experts:])

    over_y = swap(weights, 2)

    width = queries.shape[1] // groups
    lined = lax.dynamic_slice_in_dim(queries, group * width, width, axis=1)
    bit, order = planes // 2, [0]
    lined = jnp.concatenate([lined, swap(lined, bit * QUAD)], axis=0)
    order = order + [o ^ bit for o in order]

    middle = (planes + 1) // 2
    up, down = tokens, tokens
    first = []
    for s in range(1, middle):
        up, down = move(up, [(p, p + 1) for p in range(s - 1, planes - 1)]), move(
            down, [(p, p - 1) for p in range(1, planes - s + 1)]
        )
        first.extend([up, down])
    over_core = swap(weights, 1)
    lined = after(lined, wide, wide_late, *first)
    bit //= 2
    while bit:
        lined = jnp.concatenate([lined, swap(lined, bit * QUAD)], axis=0)
        order = order + [o ^ bit for o in order]
        bit //= 2

    for s in range(middle, planes):
        up_hops = [(p, p + 1) for p in range(s - 1, planes - 1)]
        down_hops = [(p, p - 1) for p in range(1, planes - s + 1)]
        if s == middle:
            up, down = move(up, up_hops), move(down, down_hops)
            up = down = up + after(down, lined)
            across = swap(after(over_y, up), 1)
            quad_weights = [weights, over_core, over_y, across]
            lined = after(lined, up)
            ranged = [lined] + [
                lax.ppermute(lined, "groups", [(g, (g + k) % groups) for g in range(groups)]) for k in range(1, groups)
            ]
            own, *sides = project([tokens] + first + [up], token_count, quad_weights)
            returned = [move(side, home) for side, home in zip(sides, ways_home)]
            mine = jnp.concatenate(after(tuple(ranged), own), axis=1)
            mine_over_y = swap(mine, 2)
        else:
            up = down = move(up, up_hops + down_hops)
            wait = returned if s == planes - 1 else []
            (side,) = project([after(up, *wait)], token_count, quad_weights)
            returned.append(move(side, ways_home[len(returned)]))
    late = returned.pop()
    early = combine([own] + returned, wide)

    rest = swap(after(jnp.concatenate([mine, mine_over_y], axis=0), side), 1)
    here = jnp.stack([plane, spot, group]).astype(jnp.int32)
    all_queries = assemble(here, mine, mine_over_y, rest, order, groups)
    sketches = combine([late], wide_late, early, counts)
    sketches = sketches.reshape(EX_DEV, RANK * RANK)
    scores = lax.dot_general(sketches.astype(jnp.bfloat16), all_queries, NT, preferred_element_type=jnp.float32)
    return (sketches, scores)


def solution(mesh):
    placed = (
        P(("groups", "expert"), None),
        P(("groups", "expert"), None),
        P(("groups", "expert"), None),
        P(("groups", "expert"), None),
        P(("groups", "expert"), None),
        P("expert", None, None),
        P(),
        P("expert", None),
    )
    return jax.shard_map(
        shards,
        mesh=mesh,
        in_specs=placed,
        out_specs=(P(("groups", "expert"), None), P(("groups", "expert"), None)),
        check_vma=False,
    )
```

```python
import functools
import math

import jax
import jax.numpy as jnp
from jax import lax
from jax.experimental import pallas as pl
from jax.experimental.pallas import tpu as pltpu
from jax.sharding import PartitionSpec as P

RANK = 64
EX_DEV = 4
QUAD = 4
SLAB = 16

SMALL = pl.CostEstimate(flops=1024, bytes_accessed=1024, transcendentals=0)

NT = (((1,), (1,)), ((), ()))
TN = (((0,), (0,)), ((), ()))


def room(*arrays):
    return sum(math.prod(a.shape) * jnp.dtype(a.dtype).itemsize for a in arrays) + (6 << 20)


def combine_kernel(blocks, experts, first, last, *refs):
    sides, wide = refs[:blocks], refs[blocks]
    total = jnp.zeros((RANK, EX_DEV * RANK), jnp.float32) if first else refs[blocks + 1][...]
    out = refs[-1]
    span = experts * RANK
    for b in range(blocks):
        slabs = [sides[b][:, g * span : (g + 1) * span] for g in range(wide.shape[1] // SLAB)]
        side = jnp.concatenate(slabs, axis=0)
        for e in range(experts):
            total += lax.dot_general(
                side[:, e * RANK : (e + 1) * RANK],
                wide[b * experts + e],
                TN,
                preferred_element_type=jnp.float32,
            )
    if last:
        counts = refs[-2]
        for x in range(EX_DEV):
            out[x] = total[:, x * RANK : (x + 1) * RANK] / counts[x : x + 1, :]
    else:
        out[...] = total


def combine(sides, wide, total=None, counts=None):
    experts = wide.shape[0] // len(sides)
    extra = [a for a in (total, counts) if a is not None]
    shape = (RANK, EX_DEV * RANK) if counts is None else (EX_DEV, RANK, RANK)
    return pl.pallas_call(
        functools.partial(combine_kernel, len(sides), experts, total is None, counts is not None),
        out_shape=jax.ShapeDtypeStruct(shape, jnp.float32),
        in_specs=[pl.BlockSpec(memory_space=pltpu.VMEM)] * (len(sides) + 1 + len(extra)),
        out_specs=pl.BlockSpec(memory_space=pltpu.VMEM),
        cost_estimate=SMALL,
        compiler_params=pltpu.CompilerParams(vmem_limit_bytes=room(*sides, wide)),
        name="combine",
    )(*sides, wide, *extra)


def project_kernel(blocks, rows, *refs):
    parts, weights = refs[:blocks], refs[blocks : blocks + QUAD]
    outs, total = refs[blocks + QUAD : -1], refs[-1]
    depth = 1024
    total[...] = jnp.zeros_like(total)

    @pl.loop(0, parts[0].shape[1] // depth)
    def _(i):
        span = pl.ds(pl.multiple_of(i * depth, depth), depth)
        left = jnp.concatenate([p[:rows, span] for p in parts], axis=0)
        right = jnp.concatenate([w[:, span] for w in weights], axis=0)
        total[...] += lax.dot_general(left, right, NT, preferred_element_type=jnp.float32)

    width = total.shape[1]
    for b in range(blocks):
        for g in range(rows // SLAB):
            top = b * rows + g * SLAB
            outs[b][:, g * width : (g + 1) * width] = total[top : top + SLAB].astype(jnp.bfloat16)


def project(parts, rows, weights):
    width = QUAD * weights[0].shape[0]
    vmem = pl.BlockSpec(memory_space=pltpu.VMEM)
    total = jax.ShapeDtypeStruct((rows * len(parts), width), jnp.float32)
    return pl.pallas_call(
        functools.partial(project_kernel, len(parts), rows),
        out_shape=[jax.ShapeDtypeStruct((SLAB, rows // SLAB * width), jnp.bfloat16)] * len(parts),
        in_specs=[vmem] * (len(parts) + QUAD),
        out_specs=[vmem] * len(parts),
        scratch_shapes=[pltpu.VMEM(total.shape, total.dtype)],
        cost_estimate=SMALL,
        compiler_params=pltpu.CompilerParams(vmem_limit_bytes=room(*parts, *weights, total, total)),
        name="project",
    )(*parts, *weights)


def assemble_kernel(order, groups, here_ref, mine_ref, over_y_ref, rest_ref, out_ref):
    span = mine_ref.shape[0]
    rows, columns = span // len(order), out_ref.shape[1] // groups
    sources = (mine_ref, rest_ref, over_y_ref, rest_ref)
    for rel in range(QUAD):
        base = span if rel == 3 else 0
        for d, other in enumerate(order):
            home = (here_ref[0] ^ other) * QUAD + (here_ref[1] ^ rel)
            row = pl.multiple_of(home * rows, rows)
            for k in range(groups):
                column = pl.multiple_of(lax.rem(here_ref[2] + (groups - k), groups) * columns, columns)
                out_ref[pl.ds(row, rows), pl.ds(column, columns)] = sources[rel][
                    base + d * rows : base + (d + 1) * rows, k * columns : (k + 1) * columns
                ]


def assemble(here, mine, over_y, rest, order, groups):
    span, width = mine.shape
    vmem = pl.BlockSpec(memory_space=pltpu.VMEM)
    return pl.pallas_call(
        functools.partial(assemble_kernel, order, groups),
        out_shape=jax.ShapeDtypeStruct((span * QUAD, width), mine.dtype),
        in_specs=[pl.BlockSpec(memory_space=pltpu.SMEM), vmem, vmem, vmem],
        out_specs=vmem,
        cost_estimate=SMALL,
        compiler_params=pltpu.CompilerParams(vmem_limit_bytes=room(mine, mine, mine, mine, mine, over_y, rest)),
        name="assemble",
    )(here, mine, over_y, rest)


def after(array, *others):
    return lax.optimization_barrier((array, *others))[0]


def shards(tokens, out_grad, routes, route_weight, example_ids, in_proj, out_proj, queries):
    token_count, model_width = tokens.shape
    owned = in_proj.shape[0]
    n, groups = lax.axis_size("expert"), lax.axis_size("groups")
    planes = n // QUAD
    me, group = lax.axis_index("expert"), lax.axis_index("groups")
    plane, spot = me // QUAD, me % QUAD

    def move(array, hops):
        pairs = [(a * QUAD + q, b * QUAD + q) for a, b in hops for q in range(QUAD)]
        return lax.ppermute(array, "expert", pairs)

    def swap(array, bit):
        return lax.ppermute(array, "expert", [(i, i ^ bit) for i in range(n)])

    weights = jnp.swapaxes(in_proj, 1, 2).reshape(owned * RANK, model_width)

    ways_home = []
    for s in range(1, planes):
        up_home = [(p, p - s) for p in range(s, planes)]
        down_home = [(p, p + s) for p in range(planes - s)]
        ways_home.extend([up_home + down_home] if 2 * s >= planes else [up_home, down_home])

    homes = []
    for home in ways_home:
        back = -jnp.ones((), jnp.int32)
        for a, b in home:
            back = jnp.where(plane == b, a, back)
        homes.append(back)
    grad_side = jnp.dot(out_grad, out_proj, preferred_element_type=jnp.float32)
    rel = jnp.arange(QUAD, dtype=jnp.int32)
    inner = ((spot ^ rel)[:, None] * owned + jnp.arange(owned, dtype=jnp.int32)[None, :]).reshape(-1)
    place = jnp.stack([plane] + homes)
    expert_ids = jnp.where(place[:, None] >= 0, place[:, None] * (QUAD * owned) + inner[None, :], -1).reshape(-1)
    gate = jnp.sum(
        jnp.where(routes.T[None, :, :] == expert_ids[:, None, None], route_weight.T[None, :, :], 0.0), axis=1
    )
    local_ids = example_ids.reshape(token_count)
    member = local_ids[:, None] == jnp.arange(EX_DEV, dtype=jnp.int32)[None, :]
    counts = jnp.sum(member.astype(jnp.float32), axis=0)
    counts = jnp.broadcast_to(counts[:, None], (EX_DEV, RANK))
    repeated = jnp.concatenate([grad_side] * EX_DEV, axis=1)
    widely = jnp.repeat(member, RANK, axis=1)
    experts = QUAD * owned

    def widen(part):
        spread = (part[:, :, None] * repeated[None]).astype(jnp.bfloat16)
        return jnp.where(widely[None], spread, jnp.zeros((), jnp.bfloat16))

    wide, wide_late = widen(gate[:-experts]), widen(gate[-experts:])

    over_y = swap(weights, 2)

    width = queries.shape[1] // groups
    lined = lax.dynamic_slice_in_dim(queries, group * width, width, axis=1)
    bit, order = planes // 2, [0]
    lined = jnp.concatenate([lined, swap(lined, bit * QUAD)], axis=0)
    order = order + [o ^ bit for o in order]

    middle = (planes + 1) // 2
    up, down = tokens, tokens
    first = []
    for s in range(1, middle):
        up, down = move(up, [(p, p + 1) for p in range(s - 1, planes - 1)]), move(
            down, [(p, p - 1) for p in range(1, planes - s + 1)]
        )
        first.extend([up, down])
    over_core = swap(weights, 1)
    lined = after(lined, wide, wide_late, *first)
    bit //= 2
    while bit:
        lined = jnp.concatenate([lined, swap(lined, bit * QUAD)], axis=0)
        order = order + [o ^ bit for o in order]
        bit //= 2

    for s in range(middle, planes):
        up_hops = [(p, p + 1) for p in range(s - 1, planes - 1)]
        down_hops = [(p, p - 1) for p in range(1, planes - s + 1)]
        if s == middle:
            up, down = move(up, up_hops), move(down, down_hops)
            up = down = up + after(down, lined)
            across = swap(after(over_y, up), 1)
            quad_weights = [weights, over_core, over_y, across]
            lined = after(lined, up)
            ranged = [lined] + [
                lax.ppermute(lined, "groups", [(g, (g + k) % groups) for g in range(groups)]) for k in range(1, groups)
            ]
            own, *sides = project([tokens] + first + [up], token_count, quad_weights)
            returned = [move(side, home) for side, home in zip(sides, ways_home)]
            mine = jnp.concatenate(after(tuple(ranged), own), axis=1)
            mine_over_y = swap(mine, 2)
        else:
            up = down = move(up, up_hops + down_hops)
            wait = returned if s == planes - 1 else []
            (side,) = project([after(up, *wait)], token_count, quad_weights)
            returned.append(move(side, ways_home[len(returned)]))
    late = returned.pop()
    early = combine([own] + returned, wide)

    rest = swap(after(jnp.concatenate([mine, mine_over_y], axis=0), side), 1)
    here = jnp.stack([plane, spot, group]).astype(jnp.int32)
    all_queries = assemble(here, mine, mine_over_y, rest, order, groups)
    sketches = combine([late], after(wide_late, all_queries), early, counts)
    sketches = sketches.reshape(EX_DEV, RANK * RANK)
    scores = lax.dot_general(sketches.astype(jnp.bfloat16), all_queries, NT, preferred_element_type=jnp.float32)
    return (sketches, scores)


def solution(mesh):
    placed = (
        P(("groups", "expert"), None),
        P(("groups", "expert"), None),
        P(("groups", "expert"), None),
        P(("groups", "expert"), None),
        P(("groups", "expert"), None),
        P("expert", None, None),
        P(),
        P("expert", None),
    )
    return jax.shard_map(
        shards,
        mesh=mesh,
        in_specs=placed,
        out_specs=(P(("groups", "expert"), None), P(("groups", "expert"), None)),
        check_vma=False,
    )
```

```python
import functools
import math

import jax
import jax.numpy as jnp
from jax import lax
from jax.experimental import pallas as pl
from jax.experimental.pallas import tpu as pltpu
from jax.sharding import PartitionSpec as P

RANK = 64
EX_DEV = 4
QUAD = 4
SLAB = 16

SMALL = pl.CostEstimate(flops=1024, bytes_accessed=1024, transcendentals=0)

NT = (((1,), (1,)), ((), ()))
TN = (((0,), (0,)), ((), ()))


def room(*arrays):
    return sum(math.prod(a.shape) * jnp.dtype(a.dtype).itemsize for a in arrays) + (6 << 20)


def combine_kernel(blocks, experts, first, last, *refs):
    sides, wide = refs[:blocks], refs[blocks]
    total = jnp.zeros((RANK, EX_DEV * RANK), jnp.float32) if first else refs[blocks + 1][...]
    out = refs[-1]
    span = experts * RANK
    for b in range(blocks):
        slabs = [sides[b][:, g * span : (g + 1) * span] for g in range(wide.shape[1] // SLAB)]
        side = jnp.concatenate(slabs, axis=0)
        for e in range(experts):
            total += lax.dot_general(
                side[:, e * RANK : (e + 1) * RANK],
                wide[b * experts + e],
                TN,
                preferred_element_type=jnp.float32,
            )
    if last:
        counts = refs[-2]
        for x in range(EX_DEV):
            out[x] = total[:, x * RANK : (x + 1) * RANK] / counts[x : x + 1, :]
    else:
        out[...] = total


def combine(sides, wide, total=None, counts=None):
    experts = wide.shape[0] // len(sides)
    extra = [a for a in (total, counts) if a is not None]
    shape = (RANK, EX_DEV * RANK) if counts is None else (EX_DEV, RANK, RANK)
    return pl.pallas_call(
        functools.partial(combine_kernel, len(sides), experts, total is None, counts is not None),
        out_shape=jax.ShapeDtypeStruct(shape, jnp.float32),
        in_specs=[pl.BlockSpec(memory_space=pltpu.VMEM)] * (len(sides) + 1 + len(extra)),
        out_specs=pl.BlockSpec(memory_space=pltpu.VMEM),
        cost_estimate=SMALL,
        compiler_params=pltpu.CompilerParams(vmem_limit_bytes=room(*sides, wide)),
        name="combine",
    )(*sides, wide, *extra)


def project_kernel(blocks, rows, *refs):
    parts, weights = refs[:blocks], refs[blocks : blocks + QUAD]
    outs, total = refs[blocks + QUAD : -1], refs[-1]
    depth = 1024
    total[...] = jnp.zeros_like(total)

    @pl.loop(0, parts[0].shape[1] // depth)
    def _(i):
        span = pl.ds(pl.multiple_of(i * depth, depth), depth)
        left = jnp.concatenate([p[:rows, span] for p in parts], axis=0)
        right = jnp.concatenate([w[:, span] for w in weights], axis=0)
        total[...] += lax.dot_general(left, right, NT, preferred_element_type=jnp.float32)

    width = total.shape[1]
    for b in range(blocks):
        for g in range(rows // SLAB):
            top = b * rows + g * SLAB
            outs[b][:, g * width : (g + 1) * width] = total[top : top + SLAB].astype(jnp.bfloat16)


def project(parts, rows, weights):
    width = QUAD * weights[0].shape[0]
    vmem = pl.BlockSpec(memory_space=pltpu.VMEM)
    total = jax.ShapeDtypeStruct((rows * len(parts), width), jnp.float32)
    return pl.pallas_call(
        functools.partial(project_kernel, len(parts), rows),
        out_shape=[jax.ShapeDtypeStruct((SLAB, rows // SLAB * width), jnp.bfloat16)] * len(parts),
        in_specs=[vmem] * (len(parts) + QUAD),
        out_specs=[vmem] * len(parts),
        scratch_shapes=[pltpu.VMEM(total.shape, total.dtype)],
        cost_estimate=SMALL,
        compiler_params=pltpu.CompilerParams(vmem_limit_bytes=room(*parts, *weights, total, total)),
        name="project",
    )(*parts, *weights)


def assemble_kernel(order, groups, here_ref, mine_ref, over_y_ref, rest_ref, out_ref):
    span = mine_ref.shape[0]
    rows, columns = span // len(order), out_ref.shape[1] // groups
    sources = (mine_ref, rest_ref, over_y_ref, rest_ref)
    for rel in range(QUAD):
        base = span if rel == 3 else 0
        for d, other in enumerate(order):
            home = (here_ref[0] ^ other) * QUAD + (here_ref[1] ^ rel)
            row = pl.multiple_of(home * rows, rows)
            for k in range(groups):
                column = pl.multiple_of(lax.rem(here_ref[2] + (groups - k), groups) * columns, columns)
                out_ref[pl.ds(row, rows), pl.ds(column, columns)] = sources[rel][
                    base + d * rows : base + (d + 1) * rows, k * columns : (k + 1) * columns
                ]


def assemble(here, mine, over_y, rest, order, groups):
    span, width = mine.shape
    vmem = pl.BlockSpec(memory_space=pltpu.VMEM)
    return pl.pallas_call(
        functools.partial(assemble_kernel, order, groups),
        out_shape=jax.ShapeDtypeStruct((span * QUAD, width), mine.dtype),
        in_specs=[pl.BlockSpec(memory_space=pltpu.SMEM), vmem, vmem, vmem],
        out_specs=vmem,
        cost_estimate=SMALL,
        compiler_params=pltpu.CompilerParams(vmem_limit_bytes=room(mine, mine, mine, mine, mine, over_y, rest)),
        name="assemble",
    )(here, mine, over_y, rest)


def after(array, *others):
    return lax.optimization_barrier((array, *others))[0]


def shards(tokens, out_grad, routes, route_weight, example_ids, in_proj, out_proj, queries):
    token_count, model_width = tokens.shape
    owned = in_proj.shape[0]
    n, groups = lax.axis_size("expert"), lax.axis_size("groups")
    planes = n // QUAD
    me, group = lax.axis_index("expert"), lax.axis_index("groups")
    plane, spot = me // QUAD, me % QUAD

    def move(array, hops):
        pairs = [(a * QUAD + q, b * QUAD + q) for a, b in hops for q in range(QUAD)]
        return lax.ppermute(array, "expert", pairs)

    def swap(array, bit):
        return lax.ppermute(array, "expert", [(i, i ^ bit) for i in range(n)])

    weights = jnp.swapaxes(in_proj, 1, 2).reshape(owned * RANK, model_width)

    ways_home = []
    for s in range(1, planes):
        up_home = [(p, p - s) for p in range(s, planes)]
        down_home = [(p, p + s) for p in range(planes - s)]
        ways_home.extend([up_home + down_home] if 2 * s >= planes else [up_home, down_home])

    homes = []
    for home in ways_home:
        back = -jnp.ones((), jnp.int32)
        for a, b in home:
            back = jnp.where(plane == b, a, back)
        homes.append(back)
    grad_side = jnp.dot(out_grad, out_proj, preferred_element_type=jnp.float32)
    rel = jnp.arange(QUAD, dtype=jnp.int32)
    inner = ((spot ^ rel)[:, None] * owned + jnp.arange(owned, dtype=jnp.int32)[None, :]).reshape(-1)
    place = jnp.stack([plane] + homes)
    expert_ids = jnp.where(place[:, None] >= 0, place[:, None] * (QUAD * owned) + inner[None, :], -1).reshape(-1)
    gate = jnp.sum(
        jnp.where(routes.T[None, :, :] == expert_ids[:, None, None], route_weight.T[None, :, :], 0.0), axis=1
    )
    local_ids = example_ids.reshape(token_count)
    member = local_ids[:, None] == jnp.arange(EX_DEV, dtype=jnp.int32)[None, :]
    counts = jnp.sum(member.astype(jnp.float32), axis=0)
    counts = jnp.broadcast_to(counts[:, None], (EX_DEV, RANK))
    repeated = jnp.concatenate([grad_side] * EX_DEV, axis=1)
    widely = jnp.repeat(member, RANK, axis=1)
    experts = QUAD * owned

    def widen(part):
        spread = (part[:, :, None] * repeated[None]).astype(jnp.bfloat16)
        return jnp.where(widely[None], spread, jnp.zeros((), jnp.bfloat16))

    wide, wide_late = widen(gate[:-experts]), widen(gate[-experts:])

    over_y = swap(weights, 2)

    width = queries.shape[1] // groups
    lined = lax.dynamic_slice_in_dim(queries, group * width, width, axis=1)
    bit, order = planes // 2, [0]
    lined = jnp.concatenate([lined, swap(lined, bit * QUAD)], axis=0)
    order = order + [o ^ bit for o in order]

    middle = (planes + 1) // 2
    up, down = tokens, tokens
    first = []
    for s in range(1, middle):
        up, down = move(up, [(p, p + 1) for p in range(s - 1, planes - 1)]), move(
            down, [(p, p - 1) for p in range(1, planes - s + 1)]
        )
        first.extend([up, down])
    over_core = swap(weights, 1)
    lined = after(lined, wide, wide_late, *first)
    bit //= 2
    while bit:
        lined = jnp.concatenate([lined, swap(lined, bit * QUAD)], axis=0)
        order = order + [o ^ bit for o in order]
        bit //= 2

    for s in range(middle, planes):
        up_hops = [(p, p + 1) for p in range(s - 1, planes - 1)]
        down_hops = [(p, p - 1) for p in range(1, planes - s + 1)]
        if s == middle:
            up, down = move(up, up_hops), move(down, down_hops)
            up = down = up + after(down, lined)
            across = swap(after(over_y, up), 1)
            quad_weights = [weights, over_core, over_y, across]
            lined = after(lined, up)
            ranged = [lined] + [
                lax.ppermute(lined, "groups", [(g, (g + k) % groups) for g in range(groups)]) for k in range(1, groups)
            ]
            own, *sides = project([tokens] + first + [up], token_count, quad_weights)
            returned = [move(side, home) for side, home in zip(sides, ways_home)]
            mine = jnp.concatenate(after(tuple(ranged), own), axis=1)
            mine_over_y = swap(mine, 2)
            both = jnp.concatenate([mine, mine_over_y], axis=0)
        else:
            up = down = move(up, up_hops + down_hops)
            wait = [*returned, both] if s == planes - 1 else []
            (side,) = project([after(up, *wait)], token_count, quad_weights)
            returned.append(move(side, ways_home[len(returned)]))
    late = returned.pop()
    early = combine([own] + returned, wide)

    rest = swap(after(both, side), 1)
    here = jnp.stack([plane, spot, group]).astype(jnp.int32)
    all_queries = assemble(here, mine, mine_over_y, rest, order, groups)
    sketches = combine([late], after(wide_late, all_queries), early, counts)
    sketches = sketches.reshape(EX_DEV, RANK * RANK)
    scores = lax.dot_general(sketches.astype(jnp.bfloat16), all_queries, NT, preferred_element_type=jnp.float32)
    return (sketches, scores)


def solution(mesh):
    placed = (
        P(("groups", "expert"), None),
        P(("groups", "expert"), None),
        P(("groups", "expert"), None),
        P(("groups", "expert"), None),
        P(("groups", "expert"), None),
        P("expert", None, None),
        P(),
        P("expert", None),
    )
    return jax.shard_map(
        shards,
        mesh=mesh,
        in_specs=placed,
        out_specs=(P(("groups", "expert"), None), P(("groups", "expert"), None)),
        check_vma=False,
    )
```
